256 devices in a mesh: row: 32 (over y, x, core), col: 8 (over z).
Axes of the slice: x: 4, y: 4, z: 8, core: 2. Of those that a mesh axis runs over, the one named last changes fastest.
Arguments:
- inputs: bfloat16 [1024, 8192], P('row', 'col'), may hold values from -6 to 6
- cotangent: bfloat16 [1024, 8192], P('row', 'col'), may hold values from -6 to 6
- gate_weight: bfloat16 [8192, 16384], P('col', 'row'), may hold values from -50 to 50
- up_weight: bfloat16 [8192, 16384], P('col', 'row'), may hold values from -50 to 50
- down_weight: bfloat16 [16384, 8192], P('row', 'col'), may hold values from -50 to 50
- gate_first: bfloat16 [8192, 16384], P('col', 'row'), may hold values from -15 to 15
- up_first: bfloat16 [8192, 16384], P('col', 'row'), may hold values from -15 to 15
- down_first: bfloat16 [16384, 8192], P('row', 'col'), may hold values from -15 to 15
- gate_second: bfloat16 [8192, 16384], P('col', 'row'), may hold values from 0.0099487305 to 1
- up_second: bfloat16 [8192, 16384], P('col', 'row'), may hold values from 0.0099487305 to 1
- down_second: bfloat16 [16384, 8192], P('row', 'col'), may hold values from 0.0099487305 to 1
Outputs:
- outputs: float32 [1024, 8192], P('row', 'col')
- input_grad: float32 [1024, 8192], P('row', 'col')
- step_gate: bfloat16 [8192, 16384], P('col', 'row')
- step_up: bfloat16 [8192, 16384], P('col', 'row')
- step_down: bfloat16 [16384, 8192], P('row', 'col')
The draws below stay inside these ranges and needn't reach their ends.
All inputs are finite; a program needn't handle non-finite values.
Results may differ from the reference program's by a relative error of at most 0.03.
Values may be sent and summed in bfloat16 or wider, within the bound.
No kernel may reach another device: no remote copies, remote signals or barrier semaphores. Data moves between devices by JAX's collectives and lax.ppermute only.
A program may use at most 128 MiB of HBM per device.

```python
import math
import jax
import jax.numpy as jnp
from jax import lax

D = 8192
FF = 16384
TOKENS = 1024
N_ROW = 32
N_COL = 8


def spread_out(factor_key, base, scale, slope, units_dim):
    row_key, column_key = jax.random.split(factor_key)
    row_factor = jnp.exp(jax.random.uniform(row_key, (base.shape[0], 1), jnp.float32, -0.9, 0.9))
    column_factor = jnp.exp(jax.random.uniform(column_key, (1, base.shape[1]), jnp.float32, -0.9, 0.9))
    count = base.shape[units_dim]
    position = jnp.arange(count, dtype=jnp.float32) / count - 0.5
    if units_dim == 0:
        ramp = jnp.exp(slope * position).reshape(count, 1)
    else:
        ramp = jnp.exp(slope * position).reshape(1, count)
    return base * row_factor * column_factor * ramp * scale


def draw_gate_weight(key, part):
    key = jax.random.fold_in(key, 11)
    entry_key, factor_key = jax.random.split(key)
    base = jnp.clip(jax.random.normal(entry_key, (D, FF), jnp.float32), -5.0, 5.0)
    slope = 0.92
    return spread_out(factor_key, base, 1.0, slope, 1).astype(jnp.bfloat16)


def draw_up_weight(key, part):
    key = jax.random.fold_in(key, 12)
    entry_key, factor_key = jax.random.split(key)
    base = jnp.clip(jax.random.normal(entry_key, (D, FF), jnp.float32), -5.0, 5.0)
    slope = 0.92
    return spread_out(factor_key, base, 1.0, slope, 1).astype(jnp.bfloat16)


def draw_down_weight(key, part):
    key = jax.random.fold_in(key, 13)
    entry_key, factor_key = jax.random.split(key)
    base = jnp.clip(jax.random.normal(entry_key, (FF, D), jnp.float32), -5.0, 5.0)
    slope = 0.92
    return spread_out(factor_key, base, 1.0, slope, 0).astype(jnp.bfloat16)


def draw_gate_first(key, part):
    key = jax.random.fold_in(key, 21)
    entry_key, factor_key = jax.random.split(key)
    base = jnp.clip(jax.random.normal(entry_key, (D, FF), jnp.float32), -5.0, 5.0)
    slope = -0.92
    return spread_out(factor_key, base, 0.3, slope, 1).astype(jnp.bfloat16)


def draw_up_first(key, part):
    key = jax.random.fold_in(key, 22)
    entry_key, factor_key = jax.random.split(key)
    base = jnp.clip(jax.random.normal(entry_key, (D, FF), jnp.float32), -5.0, 5.0)
    slope = -0.92
    return spread_out(factor_key, base, 0.3, slope, 1).astype(jnp.bfloat16)


def draw_down_first(key, part):
    key = jax.random.fold_in(key, 23)
    entry_key, factor_key = jax.random.split(key)
    base = jnp.clip(jax.random.normal(entry_key, (FF, D), jnp.float32), -5.0, 5.0)
    slope = -0.92
    return spread_out(factor_key, base, 0.3, slope, 0).astype(jnp.bfloat16)


def shard_levels(stream_key, shape, cuts, smallest, largest):
    level, own = 1.0, jax.random.fold_in(stream_key, 6)
    for dim, blocks in cuts:
        draws = jnp.exp(jax.random.uniform(jax.random.fold_in(own, dim), (blocks,), jnp.float32, smallest / len(cuts), largest / len(cuts)))
        level = level * jnp.repeat(draws, shape[dim] // blocks).reshape([-1 if axis == dim else 1 for axis in range(len(shape))])
    return level


def centred(key, extent, scale, bound, pieces=(), kind=jnp.bfloat16):
    array = scale * jax.random.normal(key, extent, jnp.float32)
    if pieces:
        array = array * shard_levels(key, extent, pieces, -0.22, 0.18)
    return jnp.clip(array, -bound, bound).astype(kind)


def setup_inputs(seed: int = 0) -> dict:
    key_list = jax.random.split(jax.random.key(seed), 12)
    inputs = centred(key_list[0], (TOKENS, D), 1.0, 6.0, ((0, 32), (1, 8)))
    cotangent = centred(key_list[1], (TOKENS, D), 1.0, 6.0, ((0, 32), (1, 8)))
    gate_weight = draw_gate_weight(jax.random.fold_in(key_list[11], 71), 0)
    up_weight = draw_up_weight(jax.random.fold_in(key_list[11], 71), 0)
    down_weight = draw_down_weight(jax.random.fold_in(key_list[11], 71), 0)
    gate_first = draw_gate_first(jax.random.fold_in(key_list[11], 71), 0)
    up_first = draw_up_first(jax.random.fold_in(key_list[11], 71), 0)
    down_first = draw_down_first(jax.random.fold_in(key_list[11], 71), 0)
    gate_second = jnp.clip(jnp.exp(math.log(1.0) - 4.61031033 * jax.random.uniform(key_list[8], (D, FF), jnp.float32) ** shard_levels(key_list[8], (D, FF), ((0, 8), (1, 32)), -0.2, 0.2)), 0.0099487305, 1.0).astype(jnp.bfloat16)
    up_second = jnp.clip(jnp.exp(math.log(1.0) - 4.61031033 * jax.random.uniform(key_list[9], (D, FF), jnp.float32) ** shard_levels(key_list[9], (D, FF), ((0, 8), (1, 32)), -0.2, 0.2)), 0.0099487305, 1.0).astype(jnp.bfloat16)
    down_second = jnp.clip(jnp.exp(math.log(1.0) - 4.61031033 * jax.random.uniform(key_list[10], (FF, D), jnp.float32) ** shard_levels(key_list[10], (FF, D), ((0, 32), (1, 8)), -0.2, 0.2)), 0.0099487305, 1.0).astype(jnp.bfloat16)
    return {"inputs": inputs, "cotangent": cotangent, "gate_weight": gate_weight, "up_weight": up_weight, "down_weight": down_weight, "gate_first": gate_first, "up_first": up_first, "down_first": down_first, "gate_second": gate_second, "up_second": up_second, "down_second": down_second}


FIRST_FIX = 1.0 - 0.9 ** 20
SECOND_FIX = 1.0 - 0.95 ** 20

def direction(weight, gradient, first_moment, second_moment):
    first_new = 0.9 * first_moment.astype(jnp.float32) + 0.1 * gradient
    second_new = 0.95 * second_moment.astype(jnp.float32) + 0.05 * gradient * gradient
    return first_new / FIRST_FIX / (jnp.sqrt(second_new / SECOND_FIX) + 1e-06) + 0.1 * weight.astype(jnp.float32)

def squares_of(values):
    wide = values.astype(jnp.float32)
    return jnp.sum(wide * wide)

def trusted(update, weight):
    return (jnp.sqrt(squares_of(weight) / (jnp.sum(update * update) + 1e-06)) * update).astype(jnp.bfloat16)

def block_term(left, right, transposed):
    if transposed:
        return lax.dot_general(left, right, (((1,), (1,)), ((), ())), preferred_element_type=jnp.float32)
    return jnp.dot(left, right, preferred_element_type=jnp.float32)

def rounded_block_sum(pairs, transposed, out_shape):

    def add_block(total, blocks):
        term = jnp.zeros(out_shape, jnp.float32)
        for index in range(len(blocks) // 2):
            term = term + block_term(blocks[2 * index], blocks[2 * index + 1], transposed)
        narrow = lax.optimization_barrier(term.astype(jnp.bfloat16))
        return (total + narrow.astype(jnp.float32), None)
    total, unused = lax.scan(add_block, jnp.zeros(out_shape, jnp.float32), pairs)
    return total

def reference(inputs, cotangent, gate_weight, up_weight, down_weight, gate_first, up_first, down_first, gate_second, up_second, down_second):
    width_scale = 1.0 / math.sqrt(D)
    hidden_scale = 1.0 / math.sqrt(FF)
    feat_block = D // N_COL
    unit_block = FF // N_ROW
    input_blocks = inputs.reshape(TOKENS, N_COL, feat_block).transpose(1, 0, 2)
    cotangent_blocks = cotangent.reshape(TOKENS, N_COL, feat_block).transpose(1, 0, 2)
    gate_feat = gate_weight.reshape(N_COL, feat_block, FF)
    up_feat = up_weight.reshape(N_COL, feat_block, FF)
    down_feat = down_weight.reshape(FF, N_COL, feat_block).transpose(1, 0, 2)
    gate_value = rounded_block_sum((input_blocks, gate_feat), False, (TOKENS, FF)) * width_scale
    up_value = rounded_block_sum((input_blocks, up_feat), False, (TOKENS, FF)) * width_scale
    grad_hidden = rounded_block_sum((cotangent_blocks, down_feat), True, (TOKENS, FF)) * hidden_scale
    sigmoid_gate = jax.nn.sigmoid(gate_value)
    activated = gate_value * sigmoid_gate
    hidden = (activated * up_value).astype(jnp.bfloat16)
    d_up = (grad_hidden * activated).astype(jnp.bfloat16)
    d_gate = (grad_hidden * up_value * sigmoid_gate * (1.0 + gate_value * (1.0 - sigmoid_gate))).astype(jnp.bfloat16)
    hidden_blocks = hidden.reshape(TOKENS, N_ROW, unit_block).transpose(1, 0, 2)
    d_gate_blocks = d_gate.reshape(TOKENS, N_ROW, unit_block).transpose(1, 0, 2)
    d_up_blocks = d_up.reshape(TOKENS, N_ROW, unit_block).transpose(1, 0, 2)
    down_units = down_weight.reshape(N_ROW, unit_block, D)
    gate_units = gate_weight.reshape(D, N_ROW, unit_block).transpose(1, 0, 2)
    up_units = up_weight.reshape(D, N_ROW, unit_block).transpose(1, 0, 2)
    outputs = rounded_block_sum((hidden_blocks, down_units), False, (TOKENS, D)) * hidden_scale
    input_grad = rounded_block_sum((d_gate_blocks, gate_units, d_up_blocks, up_units), True, (TOKENS, D)) * width_scale
    grad_gate = jnp.dot(inputs.T, d_gate, preferred_element_type=jnp.float32) * width_scale
    grad_up = jnp.dot(inputs.T, d_up, preferred_element_type=jnp.float32) * width_scale
    grad_down = jnp.dot(hidden.T, cotangent, preferred_element_type=jnp.float32) * hidden_scale
    update_gate = direction(gate_weight, grad_gate, gate_first, gate_second)
    update_up = direction(up_weight, grad_up, up_first, up_second)
    update_down = direction(down_weight, grad_down, down_first, down_second)
    return (outputs, input_grad, trusted(update_gate, gate_weight), trusted(update_up, up_weight), trusted(update_down, down_weight))
```

```python
import math

import jax
import jax.numpy as jnp
from jax import lax
from jax.sharding import PartitionSpec as P

D = 8192
FF = 16384
FIRST_FIX = 1.0 - 0.9**20
SECOND_FIX = 1.0 - 0.95**20
BF = jnp.bfloat16
F32 = jnp.float32


def place(y, x, core):
    return ((y % 4) * 4 + (x % 4)) * 2 + core


CHIPS = [(y, x, core) for y in range(4) for x in range(4) for core in range(2)]
SWAP = [(place(y, x, c), place(y, x, 1 - c)) for y, x, c in CHIPS]


def first_axis(step):
    return [
        (place(y, x, c), place(y, x + step, c) if c == 0 else place(y + step, x, c))
        for y, x, c in CHIPS
    ]


def second_axis(step):
    return [
        (place(y, x, c), place(y + step, x, c) if c == 0 else place(y, x + step, c))
        for y, x, c in CHIPS
    ]


def swap(values):
    return lax.ppermute(values, "row", SWAP)


def along_first(values, step):
    return lax.ppermute(values, "row", first_axis(step))


def along_second(values, step):
    return lax.ppermute(values, "row", second_axis(step))


def along_col(values, step):
    return lax.ppermute(values, "col", [(z, (z + step) % 8) for z in range(8)])


def product(left, right):
    return jnp.dot(left, right, preferred_element_type=F32)


def product_nt(left, right):
    return lax.dot_general(left, right, (((1,), (1,)), ((), ())), preferred_element_type=F32)


def product_tn(left, right):
    return lax.dot_general(left, right, (((0,), (0,)), ((), ())), preferred_element_type=F32)


def add(*terms):
    total = terms[0].astype(F32)
    for term in terms[1:]:
        total = total + term.astype(F32)
    return total


def local_grads(gate_value, up_value, grad_hidden):
    sigmoid_gate = jax.nn.sigmoid(gate_value)
    activated = gate_value * sigmoid_gate
    hidden = (activated * up_value).astype(BF)
    d_up = (grad_hidden * activated).astype(BF)
    d_gate = (
        grad_hidden * up_value * sigmoid_gate * (1.0 + gate_value * (1.0 - sigmoid_gate))
    ).astype(BF)
    return (hidden, d_gate, d_up)


def direction(weight, gradient, first_moment, second_moment):
    first_new = 0.9 * first_moment.astype(F32) + 0.1 * gradient
    second_new = 0.95 * second_moment.astype(F32) + 0.05 * gradient * gradient
    return first_new / FIRST_FIX / (
        jnp.sqrt(second_new / SECOND_FIX) + 1e-06
    ) + 0.1 * weight.astype(F32)


def squares_of(values):
    wide = values.astype(F32)
    return jnp.sum(wide * wide)


def trusted(update, weight_sq, update_sq):
    return (jnp.sqrt(weight_sq / (update_sq + 1e-06)) * update).astype(BF)


def col_scatter(part, z):
    half = part.shape[1] // 2

    def block(offset):
        return lax.dynamic_index_in_dim(part, (z + offset + 8) % 8, 0, keepdims=False)

    far = block(4)
    down = along_col(far[:half], -1)
    up = along_col(far[half:], 1)
    own_down, own_up = block(-3), block(3)
    down = jnp.concatenate([add(down, own_down[:half]).astype(BF), own_down[half:]], axis=0)
    up = jnp.concatenate([own_up[:half], add(up, own_up[half:]).astype(BF)], axis=0)
    for distance in (2, 1):
        down, up = along_col(down, -1), along_col(up, 1)
        down = add(down, block(-distance)).astype(BF)
        up = add(up, block(distance)).astype(BF)
    down, up = along_col(down, -1), along_col(up, 1)
    return add(block(0), down, up)


def col_gather(own, z):
    half = own.shape[0] // 2
    low, high = [own], [own]
    for _ in range(3):
        low.append(along_col(low[-1], 1))
        high.append(along_col(high[-1], -1))
    far = jnp.concatenate(
        [along_col(low[-1][:half], 1), along_col(high[-1][half:], -1)], axis=0
    )
    ring = jnp.stack([own, high[1], high[2], high[3], far, low[3], low[2], low[1]])
    return jnp.roll(ring, z, axis=0)


def total_over_all(sums):
    row = jnp.stack(sums).reshape(1, len(sums))
    for axis, size in (("row", 32), ("col", 8)):
        wide = jnp.broadcast_to(row, (size, row.shape[1]))
        row = jnp.sum(lax.all_to_all(wide, axis, 0, 0, tiled=True), axis=0, keepdims=True)
    return row[0]


def local(
    inputs,
    cotangent,
    gate_weight,
    up_weight,
    down_weight,
    gate_first,
    up_first,
    down_first,
    gate_second,
    up_second,
    down_second,
):
    width_scale = 1.0 / math.sqrt(D)
    hidden_scale = 1.0 / math.sqrt(FF)
    core = lax.axis_index("row") % 2
    z = lax.axis_index("col")

    both = jnp.stack([inputs, cotangent])
    own = lax.dynamic_slice_in_dim(both, core * 16, 16, axis=1)
    other = lax.dynamic_slice_in_dim(both, (1 - core) * 16, 16, axis=1)
    chip = jnp.concatenate([own, swap(other)], axis=1)
    line = jnp.concatenate(
        [chip, along_first(chip, -1), along_first(chip, 2), along_first(chip, 1)], axis=1
    )
    lines = [line, along_second(line, -1), along_second(line, 2), along_second(line, 1)]

    gate_up = jnp.concatenate([gate_weight, up_weight], axis=1)
    tokens, hiddens, grads, out_parts = [], [], [], []
    for stream in (0, 1):
        mine = jnp.concatenate(lines[2 * stream : 2 * stream + 2], axis=1)
        gathered = jnp.concatenate([mine, swap(mine)], axis=1)
        tokens.append(gathered)
        part = jnp.concatenate(
            [
                product(gathered[0], gate_up).astype(BF),
                product_nt(gathered[1], down_weight).astype(BF),
            ],
            axis=1,
        )
        sums = col_scatter(part.reshape(8, 64, 1536), z)
        values = local_grads(
            sums[:, :512] * width_scale, sums[:, 512:1024] * width_scale, sums[:, 1024:] * hidden_scale
        )
        full = col_gather(jnp.concatenate(values, axis=1), z).reshape(512, 1536)
        hidden, grad = full[:, :512], full[:, 512:]
        hiddens.append(hidden)
        grads.append(grad)
        out = jnp.stack(
            [product(hidden, down_weight).astype(BF), product_nt(grad, gate_up).astype(BF)]
        )
        out_parts.append(add(out[:, :256], swap(out[:, 256:])).astype(BF))

    line_sum = add(
        out_parts[0][:, :128],
        along_second(out_parts[0][:, 128:], 1),
        along_second(out_parts[1][:, :128], 2),
        along_second(out_parts[1][:, 128:], -1),
    ).astype(BF)
    chip_sum = add(
        line_sum[:, :32],
        along_first(line_sum[:, 32:64], 1),
        along_first(line_sum[:, 64:96], 2),
        along_first(line_sum[:, 96:], -1),
    )
    kept, given = chip_sum[:, :16], swap(chip_sum[:, 16:])
    rows = jnp.where(
        core == 0,
        jnp.concatenate([kept, given], axis=1),
        jnp.concatenate([given, kept], axis=1),
    )
    outputs, input_grad = rows[0] * hidden_scale, rows[1] * width_scale

    all_tokens = jnp.concatenate(tokens, axis=1)
    all_hidden = jnp.concatenate(hiddens, axis=0)
    all_grads = jnp.concatenate(grads, axis=0)
    grad_gate_up = product_tn(all_tokens[0], all_grads) * width_scale
    grad_down = product_tn(all_hidden, all_tokens[1]) * hidden_scale
    update_gate = direction(gate_weight, grad_gate_up[:, :512], gate_first, gate_second)
    update_up = direction(up_weight, grad_gate_up[:, 512:], up_first, up_second)
    update_down = direction(down_weight, grad_down, down_first, down_second)
    totals = total_over_all(
        [
            squares_of(gate_weight),
            squares_of(up_weight),
            squares_of(down_weight),
            squares_of(update_gate),
            squares_of(update_up),
            squares_of(update_down),
        ]
    )
    step_gate = trusted(update_gate, totals[0], totals[3])
    step_up = trusted(update_up, totals[1], totals[4])
    step_down = trusted(update_down, totals[2], totals[5])
    return (outputs, input_grad, step_gate, step_up, step_down)


def solution(mesh):
    placed = (
        P("row", "col"),
        P("row", "col"),
        P("col", "row"),
        P("col", "row"),
        P("row", "col"),
        P("col", "row"),
        P("col", "row"),
        P("row", "col"),
        P("col", "row"),
        P("col", "row"),
        P("row", "col"),
    )
    return jax.shard_map(
        local,
        mesh=mesh,
        in_specs=placed,
        out_specs=(
            P("row", "col"),
            P("row", "col"),
            P("col", "row"),
            P("col", "row"),
            P("row", "col"),
        ),
        check_vma=False,
    )
```

```python
import functools
import math

import jax
import jax.numpy as jnp
from jax import lax
from jax.experimental import pallas as pl
from jax.experimental.pallas import tpu as pltpu
from jax.sharding import PartitionSpec as P

D = 8192
FF = 16384
FIRST_FIX = 1.0 - 0.9**20
SECOND_FIX = 1.0 - 0.95**20
BF = jnp.bfloat16
F32 = jnp.float32
ROWS = 32
WIDTH_SCALE = 1.0 / math.sqrt(D)
HIDDEN_SCALE = 1.0 / math.sqrt(FF)
ANYWHERE = pl.BlockSpec(memory_space=pl.ANY)
VMEM = pl.BlockSpec(memory_space=pltpu.VMEM)


def place(y, x, core):
    return ((y % 4) * 4 + (x % 4)) * 2 + core


CHIPS = [(y, x, core) for y in range(4) for x in range(4) for core in range(2)]
SWAP = [(place(y, x, c), place(y, x, 1 - c)) for y, x, c in CHIPS]


def first_axis(step):
    return [
        (place(y, x, c), place(y, x + step, c) if c == 0 else place(y + step, x, c))
        for y, x, c in CHIPS
    ]


def second_axis(step):
    return [
        (place(y, x, c), place(y + step, x, c) if c == 0 else place(y, x + step, c))
        for y, x, c in CHIPS
    ]


def swap(values):
    return lax.ppermute(values, "row", SWAP)


def along_first(values, step):
    return lax.ppermute(values, "row", first_axis(step))


def along_second(values, step):
    return lax.ppermute(values, "row", second_axis(step))


def along_col(values, step):
    return lax.ppermute(values, "col", [(z, (z + step) % 8) for z in range(8)])


def product(left, right):
    return jnp.dot(left, right, preferred_element_type=F32)


def product_nt(left, right):
    return lax.dot_general(left, right, (((1,), (1,)), ((), ())), preferred_element_type=F32)


def product_tn(left, right):
    return lax.dot_general(left, right, (((0,), (0,)), ((), ())), preferred_element_type=F32)


def add(*terms):
    total = terms[0].astype(F32)
    for term in terms[1:]:
        total = total + term.astype(F32)
    return total


def local_grads(gate_value, up_value, grad_hidden):
    sigmoid_gate = jax.nn.sigmoid(gate_value)
    activated = gate_value * sigmoid_gate
    hidden = (activated * up_value).astype(BF)
    d_up = (grad_hidden * activated).astype(BF)
    d_gate = (
        grad_hidden * up_value * sigmoid_gate * (1.0 + gate_value * (1.0 - sigmoid_gate))
    ).astype(BF)
    return (hidden, d_gate, d_up)


def col_scatter(part, z):
    half = part.shape[1] // 2

    def block(offset):
        return lax.dynamic_index_in_dim(part, (z + offset + 8) % 8, 0, keepdims=False)

    far = block(4)
    down = along_col(far[:half], -1)
    up = along_col(far[half:], 1)
    own_down, own_up = block(-3), block(3)
    down = jnp.concatenate([add(down, own_down[:half]).astype(BF), own_down[half:]], axis=0)
    up = jnp.concatenate([own_up[:half], add(up, own_up[half:]).astype(BF)], axis=0)
    for distance in (2, 1):
        down, up = along_col(down, -1), along_col(up, 1)
        down = add(down, block(-distance)).astype(BF)
        up = add(up, block(distance)).astype(BF)
    down, up = along_col(down, -1), along_col(up, 1)
    return add(block(0), down, up)


def col_gather(own):
    half = own.shape[0] // 2
    low, high = [own], [own]
    for _ in range(3):
        low.append(along_col(low[-1], 1))
        high.append(along_col(high[-1], -1))
    far_low, far_high = along_col(low[-1][:half], 1), along_col(high[-1][half:], -1)
    return (own, high[1], high[2], high[3], far_low, far_high, low[3], low[2], low[1])


def first_kernel(mine, theirs, gate_w, up_w, down_w, *rest):
    part = rest[-1]
    for at, rows in ((0, mine), (256, theirs)):
        part[at : at + 256, :512] = product(rows[0], gate_w[...]).astype(BF)
        part[at : at + 256, 512:1024] = product(rows[0], up_w[...]).astype(BF)
        part[at : at + 256, 1024:] = product_nt(rows[1], down_w[...]).astype(BF)


def first_products(mine, theirs, weights, after):
    return pl.pallas_call(
        first_kernel,
        in_specs=[VMEM] * 5 + [ANYWHERE],
        out_specs=VMEM,
        out_shape=jax.ShapeDtypeStruct((512, 1536), BF),
        compiler_params=pltpu.CompilerParams(vmem_limit_bytes=24 * 2**20),
        cost_estimate=pl.CostEstimate(
            flops=2 * 512 * 1024 * 1536, bytes_accessed=6 * 2**20, transcendentals=0
        ),
        name="first_products",
    )(mine, theirs, *weights, after)


def second_kernel(stream, spot, *refs):
    pieces, (gate_w, up_w, down_w) = refs[:9], refs[9:12]
    full, kept, given = refs[-3:]
    base, row = 512 * stream, 0
    for piece in pieces:
        rows = piece.shape[0]
        block = lax.rem(spot[0] + (row // 64), 8)
        start = pl.multiple_of(base + block * 64 + row % 64, 32)
        full[pl.ds(start, rows), :] = piece[...]
        row += rows
    for at, out in ((base, kept), (base + 256, given)):
        rows = slice(at, at + 256)
        out[0] = product(full[rows, :512], down_w[...]).astype(BF)
        out[1] = (
            product_nt(full[rows, 512:1024], gate_w[...])
            + product_nt(full[rows, 1024:], up_w[...])
        ).astype(BF)


def second_products(stream, spot, pieces, weights, full, after):
    operands = [spot, *pieces, *weights, *full, *after]
    return pl.pallas_call(
        functools.partial(second_kernel, stream),
        in_specs=[pl.BlockSpec(memory_space=pltpu.SMEM)]
        + [VMEM] * (12 + len(full))
        + [ANYWHERE] * len(after),
        out_specs=[VMEM] * 3,
        out_shape=[
            jax.ShapeDtypeStruct((1024, 1536), BF),
            jax.ShapeDtypeStruct((2, 256, 1024), BF),
            jax.ShapeDtypeStruct((2, 256, 1024), BF),
        ],
        input_output_aliases={13: 0} if full else {},
        compiler_params=pltpu.CompilerParams(vmem_limit_bytes=24 * 2**20),
        cost_estimate=pl.CostEstimate(
            flops=2 * 512 * 1024 * 1536, bytes_accessed=8 * 2**20, transcendentals=0
        ),
        name="second_products",
    )(*operands)


def line_kernel(own, ahead, behind, across, after, *outs):
    del after
    total = add(own[...], ahead[...], behind[...], across[...]).astype(BF)
    for index in range(4):
        outs[index][...] = total[:, 32 * index : 32 * index + 32]


def line_total(own, ahead, behind, across, after):
    piece = jax.ShapeDtypeStruct((2, 32, 1024), BF)
    return pl.pallas_call(
        line_kernel,
        in_specs=[VMEM] * 4 + [ANYWHERE],
        out_specs=[VMEM] * 4,
        out_shape=[piece] * 4,
        compiler_params=pltpu.CompilerParams(vmem_limit_bytes=16 * 2**20),
        cost_estimate=pl.CostEstimate(
            flops=3 * 2**18, bytes_accessed=3 * 2**20, transcendentals=0
        ),
        name="line_total",
    )(own, ahead, behind, across, after)


def stage_kernel(*refs):
    sources, kept, line, sums = refs[:9], refs[9:18], refs[18], refs[19]
    step = pl.program_id(0)

    @pl.when(step == 0)
    def _():
        sums[...] = jnp.zeros_like(sums)

    for source, target in zip(sources, kept):
        rows = source.shape[0]
        target[pl.ds(pl.multiple_of(step * rows, rows), rows), :] = source[...]
    for slot in range(3):
        weight = sources[slot]

        def some(index, total, weight=weight):
            rows = pl.ds(pl.multiple_of(index * ROWS, ROWS), ROWS)
            return total + folded(weight[rows, :].astype(F32))

        sums[slot] += lax.fori_loop(
            0, weight.shape[0] // ROWS, some, jnp.zeros((8, 128), F32)
        )

    @pl.when(step == 3)
    def _():
        line[...] = sums_line(sums)


def staged(arrays):
    return pl.pallas_call(
        stage_kernel,
        grid=(4,),
        in_specs=[pl.BlockSpec((a.shape[0] // 4, a.shape[1]), lambda i: (i, 0)) for a in arrays],
        out_specs=[VMEM] * 10,
        out_shape=[jax.ShapeDtypeStruct(a.shape, a.dtype) for a in arrays]
        + [jax.ShapeDtypeStruct((1, 128), F32)],
        scratch_shapes=[pltpu.VMEM((6, 8, 128), F32)],
        compiler_params=pltpu.CompilerParams(vmem_limit_bytes=24 * 2**20),
        cost_estimate=pl.CostEstimate(
            flops=2**22, bytes_accessed=9 * 2**20, transcendentals=0
        ),
        name="staged",
    )(*arrays)


def pair_kernel(first, second, after, out):
    del after
    out[:, :128] = first[...]
    out[:, 128:] = second[...]


def paired(first, second, after):
    return pl.pallas_call(
        pair_kernel,
        in_specs=[VMEM] * 2 + [ANYWHERE],
        out_specs=VMEM,
        out_shape=jax.ShapeDtypeStruct((2, 256, 1024), BF),
        compiler_params=pltpu.CompilerParams(vmem_limit_bytes=16 * 2**20),
        cost_estimate=pl.CostEstimate(
            flops=2**18, bytes_accessed=2 * 2**20, transcendentals=0
        ),
        name="paired",
    )(first, second, after)


def lay_kernel(mine_a, theirs_a, mine_b, theirs_b, after, turned, cots):
    del after
    for at, rows in ((0, mine_a), (256, theirs_a), (512, mine_b), (768, theirs_b)):
        turned[:, at : at + 256] = rows[0].T
        cots[at : at + 256, :] = rows[1]


def laid(tokens, after):
    square = jax.ShapeDtypeStruct((1024, 1024), BF)
    return pl.pallas_call(
        lay_kernel,
        in_specs=[VMEM] * 4 + [ANYWHERE],
        out_specs=[VMEM] * 2,
        out_shape=[square, square],
        compiler_params=pltpu.CompilerParams(vmem_limit_bytes=32 * 2**20),
        cost_estimate=pl.CostEstimate(
            flops=2**20, bytes_accessed=8 * 2**20, transcendentals=0
        ),
        name="laid",
    )(*tokens, after)


def moved(raw, scale, weight, first_moment, second_moment):
    first = first_moment.astype(F32) * (0.9 / FIRST_FIX) + raw * (0.1 * scale / FIRST_FIX)
    second = second_moment.astype(F32) * (0.95 / SECOND_FIX) + (raw * raw) * (
        0.05 * scale * scale / SECOND_FIX
    )
    below = second * lax.rsqrt(second) + 1e-06
    inverse = pl.reciprocal(below, approx=True)
    inverse = inverse * (2.0 - below * inverse)
    return first * inverse + 0.1 * weight.astype(F32)


def folded(values):
    squares = values * values
    total = squares[:8]
    for at in range(8, values.shape[0], 8):
        total = total + squares[at : at + 8]
    out = total[:, :128]
    for at in range(128, values.shape[1], 128):
        out = out + total[:, at : at + 128]
    return out


def moved_rows(raw, scale, w, m, v, out, lanes, base, sums, slot):
    def some(index, total):
        rows = pl.ds(pl.multiple_of(index * ROWS, ROWS), ROWS)
        there = pl.ds(pl.multiple_of(base + index * ROWS, ROWS), ROWS)
        update = moved(raw[rows, lanes], scale, w[there, :], m[there, :], v[there, :])
        out[rows if out.shape[0] == raw.shape[0] else there, lanes] = update
        return total + folded(update)

    sums[slot] += lax.fori_loop(0, raw.shape[0] // ROWS, some, jnp.zeros((8, 128), F32))


def sums_line(sums):
    lane = lax.broadcasted_iota(jnp.int32, (1, 128), 1)
    line = jnp.zeros((1, 128), F32)
    for slot in range(6):
        line = jnp.where(lane == slot, jnp.sum(sums[slot]), line)
    return line


def down_kernel(cots, full, w, m, v, weight_line, out, line, raw, sums):
    step = pl.program_id(0)

    @pl.when(step == 0)
    def _():
        sums[...] = jnp.zeros_like(sums)

    base = pl.multiple_of(step * 256, 256)
    raw[...] = product_tn(full[:, pl.ds(base, 256)], cots[...])
    moved_rows(raw, HIDDEN_SCALE, w, m, v, out, slice(0, 1024), base, sums, 5)

    @pl.when(step == 1)
    def _():
        line[...] = sums_line(sums) + weight_line[...]


def down_update(cots, full, w, m, v, weight_line):
    return pl.pallas_call(
        down_kernel,
        grid=(2,),
        in_specs=[VMEM] * 6,
        out_specs=[pl.BlockSpec((256, 1024), lambda i: (i, 0)), VMEM],
        out_shape=[
            jax.ShapeDtypeStruct((512, 1024), F32),
            jax.ShapeDtypeStruct((1, 128), F32),
        ],
        scratch_shapes=[pltpu.VMEM((256, 1024), F32), pltpu.VMEM((6, 8, 128), F32)],
        compiler_params=pltpu.CompilerParams(vmem_limit_bytes=24 * 2**20),
        cost_estimate=pl.CostEstimate(
            flops=2 * 1024 * 1024 * 512, bytes_accessed=8 * 2**20, transcendentals=0
        ),
        name="down_update",
    )(cots, full, w, m, v, weight_line)


def wide_kernel(
    turned, full, gate_w, gate_m, gate_v, up_w, up_m, up_v,
    down_line, after, out, lines, raw, sums,
):
    del after
    step = pl.program_id(0)

    @pl.when(step == 0)
    def _():
        sums[...] = jnp.zeros_like(sums)

    base = pl.multiple_of(step * 256, 256)
    raw[...] = product(turned[pl.ds(base, 256), :], full[:, 512:])
    moved_rows(raw, WIDTH_SCALE, gate_w, gate_m, gate_v, out, slice(0, 512), base, sums, 3)
    moved_rows(raw, WIDTH_SCALE, up_w, up_m, up_v, out, slice(512, 1024), base, sums, 4)

    @pl.when(step == 3)
    def _():
        lines[...] = jnp.broadcast_to(sums_line(sums) + down_line[...], lines.shape)


def wide_update(turned, full, gate, up, down_line, after):
    return pl.pallas_call(
        wide_kernel,
        grid=(4,),
        in_specs=[VMEM] * 9 + [ANYWHERE],
        out_specs=[pl.BlockSpec((256, 1024), lambda i: (i, 0)), VMEM],
        out_shape=[
            jax.ShapeDtypeStruct((1024, 1024), F32),
            jax.ShapeDtypeStruct((256, 128), F32),
        ],
        scratch_shapes=[pltpu.VMEM((256, 1024), F32), pltpu.VMEM((6, 8, 128), F32)],
        compiler_params=pltpu.CompilerParams(vmem_limit_bytes=24 * 2**20),
        cost_estimate=pl.CostEstimate(
            flops=2 * 1024 * 1024 * 1024, bytes_accessed=16 * 2**20, transcendentals=0
        ),
        name="wide_update",
    )(turned, full, *gate, *up, down_line, after)


def step_kernel(sums, wide, narrow, gate_out, up_out, down_out):
    totals = jnp.sum(sums[...], axis=0, keepdims=True)

    def ratio(slot):
        return jnp.sqrt(totals[:, slot : slot + 1] / (totals[:, slot + 3 : slot + 4] + 1e-06))

    gate_out[...] = (ratio(0) * wide[:, :512]).astype(BF)
    up_out[...] = (ratio(1) * wide[:, 512:]).astype(BF)
    down_out[...] = (ratio(2) * narrow[...]).astype(BF)


def steps(sums, wide, narrow):
    tall = pl.BlockSpec((256, 512), lambda i: (i, 0))
    flat = pl.BlockSpec((128, 1024), lambda i: (i, 0))
    return pl.pallas_call(
        step_kernel,
        grid=(4,),
        in_specs=[VMEM, pl.BlockSpec((256, 1024), lambda i: (i, 0)), flat],
        out_specs=[tall, tall, flat],
        out_shape=[
            jax.ShapeDtypeStruct((1024, 512), BF),
            jax.ShapeDtypeStruct((1024, 512), BF),
            jax.ShapeDtypeStruct((512, 1024), BF),
        ],
        compiler_params=pltpu.CompilerParams(vmem_limit_bytes=56 * 2**20),
        cost_estimate=pl.CostEstimate(
            flops=2 * 1024 * 1536, bytes_accessed=9 * 2**20, transcendentals=0
        ),
        name="steps",
    )(sums, wide, narrow)


def local(
    inputs,
    cotangent,
    gate_weight,
    up_weight,
    down_weight,
    gate_first,
    up_first,
    down_first,
    gate_second,
    up_second,
    down_second,
):
    core = lax.axis_index("row") % 2
    z = lax.axis_index("col")

    both = jnp.stack([inputs, cotangent])
    own = lax.dynamic_slice_in_dim(both, core * 16, 16, axis=1)
    other = lax.dynamic_slice_in_dim(both, (1 - core) * 16, 16, axis=1)
    chip = jnp.concatenate([own, swap(other)], axis=1)
    line = jnp.concatenate(
        [chip, along_first(chip, -1), along_first(chip, 2), along_first(chip, 1)], axis=1
    )
    ahead, behind = along_second(line, -1), along_second(line, 1)
    across = along_second(line, 2)

    *kept, weight_line = staged(
        (
            gate_weight,
            up_weight,
            down_weight,
            gate_first,
            up_first,
            down_first,
            gate_second,
            up_second,
            down_second,
        )
    )
    weights = kept[:3]
    mines = [paired(ahead, behind, weight_line), paired(line, across, weight_line)]
    theirs, pieces = [], []
    after = across
    for mine in mines:
        theirs.append(swap(mine))
        part = first_products(mine, theirs[-1], weights, after)
        after = part
        sums = col_scatter(part.reshape(8, 64, 1536), z)
        values = local_grads(
            sums[:, :512] * WIDTH_SCALE, sums[:, 512:1024] * WIDTH_SCALE, sums[:, 1024:] * HIDDEN_SCALE
        )
        pieces.append(col_gather(jnp.concatenate(values, axis=1)))
    turned, cots = laid((mines[0], theirs[0], mines[1], theirs[1]), after)

    spot = jnp.reshape(z, (1,)).astype(jnp.int32)
    full, kept_a, given_a = second_products(
        0, spot, pieces[0], weights, (), (pieces[1][3], pieces[1][6], turned)
    )
    got_a = swap(given_a)
    ahead_sum = add(kept_a[:, :128], got_a[:, :128]).astype(BF)
    behind_sum = add(kept_a[:, 128:], got_a[:, 128:]).astype(BF)
    full, kept_b, given_b = second_products(
        1, spot, pieces[1], weights, (full,), (ahead_sum, behind_sum)
    )
    got_b = swap(given_b)
    narrow, down_line = down_update(cots, full, kept[2], kept[5], kept[8], weight_line)
    own_sum = add(kept_b[:, :128], got_b[:, :128]).astype(BF)
    across_sum = add(kept_b[:, 128:], got_b[:, 128:]).astype(BF)
    wide, sums = wide_update(
        turned, full, (kept[0], kept[3], kept[6]), (kept[1], kept[4], kept[7]), down_line, across_sum
    )
    line_sums = line_total(
        own_sum,
        along_second(ahead_sum, 1),
        along_second(behind_sum, -1),
        along_second(across_sum, 2),
        sums,
    )
    chip_sum = add(
        line_sums[0],
        along_first(line_sums[1], 1),
        along_first(line_sums[2], 2),
        along_first(line_sums[3], -1),
    )
    held, given = chip_sum[:, :16], swap(chip_sum[:, 16:])
    rows = jnp.where(
        core == 0,
        jnp.concatenate([held, given], axis=1),
        jnp.concatenate([given, held], axis=1),
    )
    outputs, input_grad = rows[0] * HIDDEN_SCALE, rows[1] * WIDTH_SCALE

    sums = lax.all_to_all(sums, ("row", "col"), 0, 0, tiled=True)
    step_gate, step_up, step_down = steps(sums, wide, narrow)
    return (outputs, input_grad, step_gate, step_up, step_down)


def solution(mesh):
    placed = (
        P("row", "col"),
        P("row", "col"),
        P("col", "row"),
        P("col", "row"),
        P("row", "col"),
        P("col", "row"),
        P("col", "row"),
        P("row", "col"),
        P("col", "row"),
        P("col", "row"),
        P("row", "col"),
    )
    return jax.shard_map(
        local,
        mesh=mesh,
        in_specs=placed,
        out_specs=(
            P("row", "col"),
            P("row", "col"),
            P("col", "row"),
            P("col", "row"),
            P("row", "col"),
        ),
        check_vma=False,
    )
```

```python
import functools
import math

import jax
import jax.numpy as jnp
from jax import lax
from jax.experimental import pallas as pl
from jax.experimental.pallas import tpu as pltpu
from jax.sharding import PartitionSpec as P

D = 8192
FF = 16384
FIRST_FIX = 1.0 - 0.9**20
SECOND_FIX = 1.0 - 0.95**20
BF = jnp.bfloat16
F32 = jnp.float32
ROWS = 32
WIDTH_SCALE = 1.0 / math.sqrt(D)
HIDDEN_SCALE = 1.0 / math.sqrt(FF)
ANYWHERE = pl.BlockSpec(memory_space=pl.ANY)
VMEM = pl.BlockSpec(memory_space=pltpu.VMEM)
CHEAP = pl.CostEstimate(flops=0, bytes_accessed=0, transcendentals=0)


def place(y, x, core):
    return ((y % 4) * 4 + (x % 4)) * 2 + core


CHIPS = [(y, x, core) for y in range(4) for x in range(4) for core in range(2)]
SWAP = [(place(y, x, c), place(y, x, 1 - c)) for y, x, c in CHIPS]


def first_axis(step):
    return [
        (place(y, x, c), place(y, x + step, c) if c == 0 else place(y + step, x, c))
        for y, x, c in CHIPS
    ]


def second_axis(step):
    return [
        (place(y, x, c), place(y + step, x, c) if c == 0 else place(y, x + step, c))
        for y, x, c in CHIPS
    ]


def swap(values):
    return lax.ppermute(values, "row", SWAP)


def along_first(values, step):
    return lax.ppermute(values, "row", first_axis(step))


def along_second(values, step):
    return lax.ppermute(values, "row", second_axis(step))


def along_col(values, step):
    return lax.ppermute(values, "col", [(z, (z + step) % 8) for z in range(8)])


def product(left, right):
    return jnp.dot(left, right, preferred_element_type=F32)


def product_nt(left, right):
    return lax.dot_general(left, right, (((1,), (1,)), ((), ())), preferred_element_type=F32)


def product_tn(left, right):
    return lax.dot_general(left, right, (((0,), (0,)), ((), ())), preferred_element_type=F32)


def add(*terms):
    total = terms[0].astype(F32)
    for term in terms[1:]:
        total = total + term.astype(F32)
    return total


def local_grads(gate_value, up_value, grad_hidden):
    sigmoid_gate = jax.nn.sigmoid(gate_value)
    activated = gate_value * sigmoid_gate
    hidden = (activated * up_value).astype(BF)
    d_up = (grad_hidden * activated).astype(BF)
    d_gate = (
        grad_hidden * up_value * sigmoid_gate * (1.0 + gate_value * (1.0 - sigmoid_gate))
    ).astype(BF)
    return (hidden, d_gate, d_up)


def col_scatter(part, z):
    half = part.shape[1] // 2

    def block(offset):
        return lax.dynamic_index_in_dim(part, (z + offset + 8) % 8, 0, keepdims=False)

    far = block(4)
    down = along_col(far[:half], -1)
    up = along_col(far[half:], 1)
    own_down, own_up = block(-3), block(3)
    down = jnp.concatenate([add(down, own_down[:half]).astype(BF), own_down[half:]], axis=0)
    up = jnp.concatenate([own_up[:half], add(up, own_up[half:]).astype(BF)], axis=0)
    for distance in (2, 1):
        down, up = along_col(down, -1), along_col(up, 1)
        down = add(down, block(-distance)).astype(BF)
        up = add(up, block(distance)).astype(BF)
    down, up = along_col(down, -1), along_col(up, 1)
    return add(block(0), down, up)


def col_gather(own):
    half = own.shape[0] // 2
    low, high = [own], [own]
    for _ in range(3):
        low.append(along_col(low[-1], 1))
        high.append(along_col(high[-1], -1))
    far_low, far_high = along_col(low[-1][:half], 1), along_col(high[-1][half:], -1)
    return (own, high[1], high[2], high[3], far_low, far_high, low[3], low[2], low[1])


def first_kernel(mine, theirs, gate_w, up_w, down_w, after, part, token):
    del after
    token[...] = jnp.zeros_like(token)
    for at, rows in ((0, mine), (256, theirs)):
        part[at : at + 256, :512] = product(rows[0], gate_w[...]).astype(BF)
        part[at : at + 256, 512:1024] = product(rows[0], up_w[...]).astype(BF)
        part[at : at + 256, 1024:] = product_nt(rows[1], down_w[...]).astype(BF)


def first_products(mine, theirs, weights, after):
    return pl.pallas_call(
        first_kernel,
        in_specs=[VMEM] * 5 + [ANYWHERE],
        out_specs=[VMEM] * 2,
        out_shape=[
            jax.ShapeDtypeStruct((512, 1536), BF),
            jax.ShapeDtypeStruct((8, 128), F32),
        ],
        compiler_params=pltpu.CompilerParams(vmem_limit_bytes=8 * 2**20),
        cost_estimate=CHEAP,
        name="first_products",
    )(mine, theirs, *weights, after)


def second_kernel(stream, spot, *refs):
    pieces, (gate_w, up_w, down_w) = refs[:9], refs[9:12]
    full, kept, given = refs[-3:]
    base, row = 512 * stream, 0
    for piece in pieces:
        rows = piece.shape[0]
        block = lax.rem(spot[0] + (row // 64), 8)
        start = pl.multiple_of(base + block * 64 + row % 64, 32)
        full[pl.ds(start, rows), :] = piece[...]
        row += rows
    for at, out in ((base, kept), (base + 256, given)):
        rows = slice(at, at + 256)
        out[0] = product(full[rows, :512], down_w[...]).astype(BF)
        out[1] = (
            product_nt(full[rows, 512:1024], gate_w[...])
            + product_nt(full[rows, 1024:], up_w[...])
        ).astype(BF)


def second_products(stream, spot, pieces, weights, full, after):
    operands = [spot, *pieces, *weights, *full, *after]
    return pl.pallas_call(
        functools.partial(second_kernel, stream),
        in_specs=[pl.BlockSpec(memory_space=pltpu.SMEM)]
        + [VMEM] * (12 + len(full))
        + [ANYWHERE] * len(after),
        out_specs=[VMEM] * 3,
        out_shape=[
            jax.ShapeDtypeStruct((1024, 1536), BF),
            jax.ShapeDtypeStruct((2, 256, 1024), BF),
            jax.ShapeDtypeStruct((2, 256, 1024), BF),
        ],
        input_output_aliases={13: 0} if full else {},
        compiler_params=pltpu.CompilerParams(vmem_limit_bytes=8 * 2**20),
        cost_estimate=CHEAP,
        name="second_products",
    )(*operands)


def line_kernel(own, ahead, behind, across, after, *outs):
    del after
    total = add(own[...], ahead[...], behind[...], across[...]).astype(BF)
    for index in range(4):
        outs[index][...] = total[:, 32 * index : 32 * index + 32]


def line_total(own, ahead, behind, across, after):
    piece = jax.ShapeDtypeStruct((2, 32, 1024), BF)
    return pl.pallas_call(
        line_kernel,
        in_specs=[VMEM] * 4 + [ANYWHERE],
        out_specs=[VMEM] * 4,
        out_shape=[piece] * 4,
        compiler_params=pltpu.CompilerParams(vmem_limit_bytes=8 * 2**20),
        cost_estimate=CHEAP,
        name="line_total",
    )(own, ahead, behind, across, after)


def stage_kernel(*refs):
    sources, kept, line, sums = refs[:3], refs[3:6], refs[6], refs[7]
    step = pl.program_id(0)

    @pl.when(step == 0)
    def _():
        sums[...] = jnp.zeros_like(sums)

    for slot in range(3):
        source, target = sources[slot], kept[slot]
        base = step * source.shape[0]

        def some(index, total, source=source, target=target, base=base):
            rows = pl.ds(pl.multiple_of(index * ROWS, ROWS), ROWS)
            values = source[rows, :]
            target[pl.ds(pl.multiple_of(base + index * ROWS, ROWS), ROWS), :] = values
            return total + folded(values.astype(F32))

        sums[slot] += lax.fori_loop(
            0, source.shape[0] // ROWS, some, jnp.zeros((8, 128), F32)
        )

    @pl.when(step == 3)
    def _():
        line[...] = sums_line(sums)


def staged(arrays):
    return pl.pallas_call(
        stage_kernel,
        grid=(4,),
        in_specs=[pl.BlockSpec((a.shape[0] // 4, a.shape[1]), lambda i: (i, 0)) for a in arrays],
        out_specs=[VMEM] * 4,
        out_shape=[jax.ShapeDtypeStruct(a.shape, a.dtype) for a in arrays]
        + [jax.ShapeDtypeStruct((1, 128), F32)],
        scratch_shapes=[pltpu.VMEM((6, 8, 128), F32)],
        compiler_params=pltpu.CompilerParams(vmem_limit_bytes=8 * 2**20),
        cost_estimate=CHEAP,
        name="staged",
    )(*arrays)


def pair_kernel(first, second, after, out, token):
    del after
    token[...] = jnp.zeros_like(token)
    out[:, :128] = first[...]
    out[:, 128:] = second[...]


def paired(first, second, after):
    return pl.pallas_call(
        pair_kernel,
        in_specs=[VMEM] * 2 + [ANYWHERE],
        out_specs=[VMEM] * 2,
        out_shape=[
            jax.ShapeDtypeStruct((2, 256, 1024), BF),
            jax.ShapeDtypeStruct((8, 128), F32),
        ],
        compiler_params=pltpu.CompilerParams(vmem_limit_bytes=8 * 2**20),
        cost_estimate=CHEAP,
        name="paired",
    )(first, second, after)


def lay_kernel(mine_a, theirs_a, mine_b, theirs_b, after, turned, cots):
    del after
    for at, rows in ((0, mine_a), (256, theirs_a), (512, mine_b), (768, theirs_b)):
        turned[:, at : at + 256] = rows[0].T
        cots[at : at + 256, :] = rows[1]


def laid(tokens, after):
    square = jax.ShapeDtypeStruct((1024, 1024), BF)
    return pl.pallas_call(
        lay_kernel,
        in_specs=[VMEM] * 4 + [ANYWHERE],
        out_specs=[VMEM] * 2,
        out_shape=[square, square],
        compiler_params=pltpu.CompilerParams(vmem_limit_bytes=8 * 2**20),
        cost_estimate=CHEAP,
        name="laid",
    )(*tokens, after)


def moved(raw, scale, weight, first_moment, second_moment):
    first = first_moment.astype(F32) * (0.9 / FIRST_FIX) + raw * (0.1 * scale / FIRST_FIX)
    second = second_moment.astype(F32) * (0.95 / SECOND_FIX) + (raw * raw) * (
        0.05 * scale * scale / SECOND_FIX
    )
    below = second * lax.rsqrt(second) + 1e-06
    inverse = pl.reciprocal(below, approx=True)
    inverse = inverse * (2.0 - below * inverse)
    return first * inverse + 0.1 * weight.astype(F32)


def folded(values):
    squares = values * values
    total = squares[:8]
    for at in range(8, values.shape[0], 8):
        total = total + squares[at : at + 8]
    out = total[:, :128]
    for at in range(128, values.shape[1], 128):
        out = out + total[:, at : at + 128]
    return out


def moved_rows(raw, scale, w, m, v, out, lanes, base, sums, slot):
    def some(index, total):
        rows = pl.ds(pl.multiple_of(index * ROWS, ROWS), ROWS)
        there = pl.ds(pl.multiple_of(base + index * ROWS, ROWS), ROWS)
        update = moved(raw[rows, lanes], scale, w[there, :], m[rows, :], v[rows, :])
        out[there, lanes] = update.astype(BF)
        return total + folded(update)

    sums[slot] += lax.fori_loop(0, raw.shape[0] // ROWS, some, jnp.zeros((8, 128), F32))


def sums_line(sums):
    lane = lax.broadcasted_iota(jnp.int32, (1, 128), 1)
    line = jnp.zeros((1, 128), F32)
    for slot in range(6):
        line = jnp.where(lane == slot, jnp.sum(sums[slot]), line)
    return line


def down_kernel(cots, full, w, m, v, weight_line, out, line, raw, sums):
    step = pl.program_id(0)

    @pl.when(step == 0)
    def _():
        sums[...] = jnp.zeros_like(sums)

    base = pl.multiple_of(step * 256, 256)
    raw[...] = product_tn(full[:, pl.ds(base, 256)], cots[...])
    moved_rows(raw, HIDDEN_SCALE, w, m, v, out, slice(0, 1024), base, sums, 5)

    @pl.when(step == 1)
    def _():
        line[...] = sums_line(sums) + weight_line[...]


def down_update(cots, full, w, m, v, weight_line):
    block = pl.BlockSpec((256, 1024), lambda i: (i, 0))
    return pl.pallas_call(
        down_kernel,
        grid=(2,),
        in_specs=[VMEM] * 3 + [block] * 2 + [VMEM],
        out_specs=[VMEM] * 2,
        out_shape=[
            jax.ShapeDtypeStruct((512, 1024), BF),
            jax.ShapeDtypeStruct((1, 128), F32),
        ],
        scratch_shapes=[pltpu.VMEM((256, 1024), F32), pltpu.VMEM((6, 8, 128), F32)],
        compiler_params=pltpu.CompilerParams(vmem_limit_bytes=10 * 2**20),
        cost_estimate=CHEAP,
        name="down_update",
    )(cots, full, w, m, v, weight_line)


def wide_kernel(
    turned, full, gate_w, up_w, gate_m, gate_v, up_m, up_v,
    down_line, after, out, lines, raw, sums,
):
    del after
    step = pl.program_id(0)

    @pl.when(step == 0)
    def _():
        sums[...] = jnp.zeros_like(sums)

    base = pl.multiple_of(step * 256, 256)
    raw[...] = product(turned[pl.ds(base, 256), :], full[:, 512:])
    moved_rows(raw, WIDTH_SCALE, gate_w, gate_m, gate_v, out, slice(0, 512), base, sums, 3)
    moved_rows(raw, WIDTH_SCALE, up_w, up_m, up_v, out, slice(512, 1024), base, sums, 4)

    @pl.when(step == 3)
    def _():
        lines[...] = jnp.broadcast_to(sums_line(sums) + down_line[...], lines.shape)


def wide_update(turned, full, gate_w, up_w, moments, down_line, after):
    block = pl.BlockSpec((256, 512), lambda i: (i, 0))
    return pl.pallas_call(
        wide_kernel,
        grid=(4,),
        in_specs=[VMEM] * 4 + [block] * 4 + [VMEM, ANYWHERE],
        out_specs=[VMEM] * 2,
        out_shape=[
            jax.ShapeDtypeStruct((1024, 1024), BF),
            jax.ShapeDtypeStruct((256, 128), F32),
        ],
        scratch_shapes=[pltpu.VMEM((256, 1024), F32), pltpu.VMEM((6, 8, 128), F32)],
        compiler_params=pltpu.CompilerParams(vmem_limit_bytes=10 * 2**20),
        cost_estimate=CHEAP,
        name="wide_update",
    )(turned, full, gate_w, up_w, *moments, down_line, after)


def step_kernel(sums, wide, narrow, gate_out, up_out, down_out):
    totals = jnp.sum(sums[...], axis=0, keepdims=True)

    def ratio(slot):
        return jnp.sqrt(totals[:, slot : slot + 1] / (totals[:, slot + 3 : slot + 4] + 1e-06))

    gate_out[...] = (ratio(0) * wide[:, :512].astype(F32)).astype(BF)
    up_out[...] = (ratio(1) * wide[:, 512:].astype(F32)).astype(BF)
    down_out[...] = (ratio(2) * narrow[...].astype(F32)).astype(BF)


def steps(sums, wide, narrow):
    tall = pl.BlockSpec((256, 512), lambda i: (i, 0))
    flat = pl.BlockSpec((128, 1024), lambda i: (i, 0))
    return pl.pallas_call(
        step_kernel,
        grid=(4,),
        in_specs=[VMEM, pl.BlockSpec((256, 1024), lambda i: (i, 0)), flat],
        out_specs=[tall, tall, flat],
        out_shape=[
            jax.ShapeDtypeStruct((1024, 512), BF),
            jax.ShapeDtypeStruct((1024, 512), BF),
            jax.ShapeDtypeStruct((512, 1024), BF),
        ],
        compiler_params=pltpu.CompilerParams(vmem_limit_bytes=56 * 2**20),
        cost_estimate=CHEAP,
        name="steps",
    )(sums, wide, narrow)


def local(
    inputs,
    cotangent,
    gate_weight,
    up_weight,
    down_weight,
    gate_first,
    up_first,
    down_first,
    gate_second,
    up_second,
    down_second,
):
    core = lax.axis_index("row") % 2
    z = lax.axis_index("col")

    both = jnp.stack([inputs, cotangent])
    own = lax.dynamic_slice_in_dim(both, core * 16, 16, axis=1)
    other = lax.dynamic_slice_in_dim(both, (1 - core) * 16, 16, axis=1)
    chip = jnp.concatenate([own, swap(other)], axis=1)
    line = jnp.concatenate(
        [chip, along_first(chip, -1), along_first(chip, 2), along_first(chip, 1)], axis=1
    )
    ahead, behind = along_second(line, -1), along_second(line, 1)
    across = along_second(line, 2)

    *weights, weight_line = staged((gate_weight, up_weight, down_weight))
    mine_a, _ = paired(ahead, behind, weight_line)
    mine_b, _ = paired(line, across, weight_line)
    after = weight_line
    mines = [mine_a, mine_b]
    theirs, pieces = [], []
    for mine in mines:
        theirs.append(swap(mine))
        part, after = first_products(mine, theirs[-1], weights, after)
        sums = col_scatter(part.reshape(8, 64, 1536), z)
        values = local_grads(
            sums[:, :512] * WIDTH_SCALE, sums[:, 512:1024] * WIDTH_SCALE, sums[:, 1024:] * HIDDEN_SCALE
        )
        pieces.append(col_gather(jnp.concatenate(values, axis=1)))
    spot = jnp.reshape(z, (1,)).astype(jnp.int32)
    full, kept_a, given_a = second_products(
        0, spot, pieces[0], weights, (), (pieces[1][3], pieces[1][6])
    )
    got_a = swap(given_a)
    ahead_sum = add(kept_a[:, :128], got_a[:, :128]).astype(BF)
    behind_sum = add(kept_a[:, 128:], got_a[:, 128:]).astype(BF)
    turned, cots = laid((mines[0], theirs[0], mines[1], theirs[1]), behind_sum)
    full, kept_b, given_b = second_products(
        1, spot, pieces[1], weights, (full,), (ahead_sum, turned)
    )
    got_b = swap(given_b)
    narrow, down_line = down_update(cots, full, weights[2], down_first, down_second, weight_line)
    own_sum = add(kept_b[:, :128], got_b[:, :128]).astype(BF)
    across_sum = add(kept_b[:, 128:], got_b[:, 128:]).astype(BF)
    wide, sums = wide_update(
        turned,
        full,
        weights[0],
        weights[1],
        (gate_first, gate_second, up_first, up_second),
        down_line,
        across_sum,
    )
    line_sums = line_total(
        own_sum,
        along_second(ahead_sum, 1),
        along_second(behind_sum, -1),
        along_second(across_sum, 2),
        sums,
    )
    chip_sum = add(
        line_sums[0],
        along_first(line_sums[1], 1),
        along_first(line_sums[2], 2),
        along_first(line_sums[3], -1),
    )
    held, given = chip_sum[:, :16], swap(chip_sum[:, 16:])
    rows = jnp.where(
        core == 0,
        jnp.concatenate([held, given], axis=1),
        jnp.concatenate([given, held], axis=1),
    )
    outputs, input_grad = rows[0] * HIDDEN_SCALE, rows[1] * WIDTH_SCALE

    sums = lax.all_to_all(sums, ("row", "col"), 0, 0, tiled=True)
    step_gate, step_up, step_down = steps(sums, wide, narrow)
    return (outputs, input_grad, step_gate, step_up, step_down)


def solution(mesh):
    placed = (
        P("row", "col"),
        P("row", "col"),
        P("col", "row"),
        P("col", "row"),
        P("row", "col"),
        P("col", "row"),
        P("col", "row"),
        P("row", "col"),
        P("col", "row"),
        P("col", "row"),
        P("row", "col"),
    )
    return jax.shard_map(
        local,
        mesh=mesh,
        in_specs=placed,
        out_specs=(
            P("row", "col"),
            P("row", "col"),
            P("col", "row"),
            P("col", "row"),
            P("row", "col"),
        ),
        check_vma=False,
    )
```

```python
import functools
import math

import jax
import jax.numpy as jnp
from jax import lax
from jax.experimental import pallas as pl
from jax.experimental.pallas import tpu as pltpu
from jax.sharding import PartitionSpec as P

D = 8192
FF = 16384
FIRST_FIX = 1.0 - 0.9**20
SECOND_FIX = 1.0 - 0.95**20
BF = jnp.bfloat16
F32 = jnp.float32
ROWS = 32
WIDTH_SCALE = 1.0 / math.sqrt(D)
HIDDEN_SCALE = 1.0 / math.sqrt(FF)
ANYWHERE = pl.BlockSpec(memory_space=pl.ANY)
VMEM = pl.BlockSpec(memory_space=pltpu.VMEM)
CHEAP = pl.CostEstimate(flops=0, bytes_accessed=0, transcendentals=0)


def place(y, x, core):
    return ((y % 4) * 4 + (x % 4)) * 2 + core


CHIPS = [(y, x, core) for y in range(4) for x in range(4) for core in range(2)]
SWAP = [(place(y, x, c), place(y, x, 1 - c)) for y, x, c in CHIPS]


def first_axis(step):
    return [
        (place(y, x, c), place(y, x + step, c) if c == 0 else place(y + step, x, c))
        for y, x, c in CHIPS
    ]


def second_axis(step):
    return [
        (place(y, x, c), place(y + step, x, c) if c == 0 else place(y, x + step, c))
        for y, x, c in CHIPS
    ]


def swap(values):
    return lax.ppermute(values, "row", SWAP)


def along_first(values, step):
    return lax.ppermute(values, "row", first_axis(step))


def along_second(values, step):
    return lax.ppermute(values, "row", second_axis(step))


def along_col(values, step):
    return lax.ppermute(values, "col", [(z, (z + step) % 8) for z in range(8)])


def product(left, right):
    return jnp.dot(left, right, preferred_element_type=F32)


def product_nt(left, right):
    return lax.dot_general(left, right, (((1,), (1,)), ((), ())), preferred_element_type=F32)


def product_tn(left, right):
    return lax.dot_general(left, right, (((0,), (0,)), ((), ())), preferred_element_type=F32)


def add(*terms):
    total = terms[0].astype(F32)
    for term in terms[1:]:
        total = total + term.astype(F32)
    return total


def local_grads(gate_value, up_value, grad_hidden):
    sigmoid_gate = jax.nn.sigmoid(gate_value)
    activated = gate_value * sigmoid_gate
    hidden = (activated * up_value).astype(BF)
    d_up = (grad_hidden * activated).astype(BF)
    d_gate = (
        grad_hidden * up_value * sigmoid_gate * (1.0 + gate_value * (1.0 - sigmoid_gate))
    ).astype(BF)
    return (hidden, d_gate, d_up)


def col_scatter(part, z):
    half = part.shape[1] // 2

    def block(offset):
        return lax.dynamic_index_in_dim(part, (z + offset + 8) % 8, 0, keepdims=False)

    far = block(4)
    down = along_col(far[:half], -1)
    up = along_col(far[half:], 1)
    own_down, own_up = block(-3), block(3)
    down = jnp.concatenate([add(down, own_down[:half]).astype(BF), own_down[half:]], axis=0)
    up = jnp.concatenate([own_up[:half], add(up, own_up[half:]).astype(BF)], axis=0)
    for distance in (2, 1):
        down, up = along_col(down, -1), along_col(up, 1)
        down = add(down, block(-distance)).astype(BF)
        up = add(up, block(distance)).astype(BF)
    down, up = along_col(down, -1), along_col(up, 1)
    return add(block(0), down, up)


def col_gather(own):
    half = own.shape[0] // 2
    low, high = [own], [own]
    for _ in range(3):
        low.append(along_col(low[-1], 1))
        high.append(along_col(high[-1], -1))
    far_low, far_high = along_col(low[-1][:half], 1), along_col(high[-1][half:], -1)
    return (own, high[1], high[2], high[3], far_low, far_high, low[3], low[2], low[1])


def first_kernel(mine, theirs, gate_w, up_w, down_w, after, part, token):
    del after
    token[...] = jnp.zeros_like(token)
    for at, rows in ((0, mine), (256, theirs)):
        part[at : at + 256, :512] = product(rows[0], gate_w[...]).astype(BF)
        part[at : at + 256, 512:1024] = product(rows[0], up_w[...]).astype(BF)
        part[at : at + 256, 1024:] = product_nt(rows[1], down_w[...]).astype(BF)


def first_products(mine, theirs, weights, after):
    return pl.pallas_call(
        first_kernel,
        in_specs=[VMEM] * 5 + [ANYWHERE],
        out_specs=[VMEM] * 2,
        out_shape=[
            jax.ShapeDtypeStruct((512, 1536), BF),
            jax.ShapeDtypeStruct((8, 128), F32),
        ],
        compiler_params=pltpu.CompilerParams(vmem_limit_bytes=8 * 2**20),
        cost_estimate=CHEAP,
        name="first_products",
    )(mine, theirs, *weights, after)


def second_kernel(stream, spot, *refs):
    pieces, (gate_w, up_w, down_w) = refs[:9], refs[9:12]
    full, kept, given = refs[-3:]
    base, row = 512 * stream, 0
    for piece in pieces:
        rows = piece.shape[0]
        block = lax.rem(spot[0] + (row // 64), 8)
        start = pl.multiple_of(base + block * 64 + row % 64, 32)
        full[pl.ds(start, rows), :] = piece[...]
        row += rows
    for at, out in ((base, kept), (base + 256, given)):
        rows = slice(at, at + 256)
        out[0] = product(full[rows, :512], down_w[...]).astype(BF)
        out[1] = (
            product_nt(full[rows, 512:1024], gate_w[...])
            + product_nt(full[rows, 1024:], up_w[...])
        ).astype(BF)


def second_products(stream, spot, pieces, weights, full, after):
    operands = [spot, *pieces, *weights, *full, *after]
    return pl.pallas_call(
        functools.partial(second_kernel, stream),
        in_specs=[pl.BlockSpec(memory_space=pltpu.SMEM)]
        + [VMEM] * (12 + len(full))
        + [ANYWHERE] * len(after),
        out_specs=[VMEM] * 3,
        out_shape=[
            jax.ShapeDtypeStruct((1024, 1536), BF),
            jax.ShapeDtypeStruct((2, 256, 1024), BF),
            jax.ShapeDtypeStruct((2, 256, 1024), BF),
        ],
        input_output_aliases={13: 0} if full else {},
        compiler_params=pltpu.CompilerParams(vmem_limit_bytes=8 * 2**20),
        cost_estimate=CHEAP,
        name="second_products",
    )(*operands)


def line_kernel(own, ahead, behind, across, after, *outs):
    del after
    total = add(own[...], ahead[...], behind[...], across[...]).astype(BF)
    for index in range(4):
        outs[index][...] = total[:, 32 * index : 32 * index + 32]


def line_total(own, ahead, behind, across, after):
    piece = jax.ShapeDtypeStruct((2, 32, 1024), BF)
    return pl.pallas_call(
        line_kernel,
        in_specs=[VMEM] * 4 + [ANYWHERE],
        out_specs=[VMEM] * 4,
        out_shape=[piece] * 4,
        compiler_params=pltpu.CompilerParams(vmem_limit_bytes=8 * 2**20),
        cost_estimate=CHEAP,
        name="line_total",
    )(own, ahead, behind, across, after)


def chip_kernel(own, ahead, across, behind, after, total):
    del after
    total[...] = add(own[...], ahead[...], across[...], behind[...])


def chip_total(own, ahead, across, behind, after):
    return pl.pallas_call(
        chip_kernel,
        in_specs=[VMEM] * 5,
        out_specs=VMEM,
        out_shape=jax.ShapeDtypeStruct((2, 32, 1024), F32),
        compiler_params=pltpu.CompilerParams(vmem_limit_bytes=8 * 2**20),
        cost_estimate=CHEAP,
        name="chip_total",
    )(own, ahead, across, behind, after)


def stage_kernel(*refs):
    sources, kept, line, sums = refs[:3], refs[3:6], refs[6], refs[7]
    step = pl.program_id(0)

    @pl.when(step == 0)
    def _():
        sums[...] = jnp.zeros_like(sums)

    for slot in range(3):
        source, target = sources[slot], kept[slot]
        base = step * source.shape[0]

        def some(index, total, source=source, target=target, base=base):
            rows = pl.ds(pl.multiple_of(index * ROWS, ROWS), ROWS)
            values = source[rows, :]
            target[pl.ds(pl.multiple_of(base + index * ROWS, ROWS), ROWS), :] = values
            return total + folded(values.astype(F32))

        sums[slot] += lax.fori_loop(
            0, source.shape[0] // ROWS, some, jnp.zeros((8, 128), F32)
        )

    @pl.when(step == 3)
    def _():
        line[...] = sums_line(sums)


def staged(arrays):
    return pl.pallas_call(
        stage_kernel,
        grid=(4,),
        in_specs=[pl.BlockSpec((a.shape[0] // 4, a.shape[1]), lambda i: (i, 0)) for a in arrays],
        out_specs=[VMEM] * 4,
        out_shape=[jax.ShapeDtypeStruct(a.shape, a.dtype) for a in arrays]
        + [jax.ShapeDtypeStruct((1, 128), F32)],
        scratch_shapes=[pltpu.VMEM((6, 8, 128), F32)],
        compiler_params=pltpu.CompilerParams(vmem_limit_bytes=8 * 2**20),
        cost_estimate=CHEAP,
        name="staged",
    )(*arrays)


def pair_kernel(first, second, after, out, token):
    del after
    token[...] = jnp.zeros_like(token)
    out[:, :128] = first[...]
    out[:, 128:] = second[...]


def paired(first, second, after):
    return pl.pallas_call(
        pair_kernel,
        in_specs=[VMEM] * 2 + [ANYWHERE],
        out_specs=[VMEM] * 2,
        out_shape=[
            jax.ShapeDtypeStruct((2, 256, 1024), BF),
            jax.ShapeDtypeStruct((8, 128), F32),
        ],
        compiler_params=pltpu.CompilerParams(vmem_limit_bytes=8 * 2**20),
        cost_estimate=CHEAP,
        name="paired",
    )(first, second, after)


def lay_kernel(mine_a, theirs_a, mine_b, theirs_b, after, turned, cots):
    del after
    for at, rows in ((0, mine_a), (256, theirs_a), (512, mine_b), (768, theirs_b)):
        turned[:, at : at + 256] = rows[0].T
        cots[at : at + 256, :] = rows[1]


def laid(tokens, after):
    square = jax.ShapeDtypeStruct((1024, 1024), BF)
    return pl.pallas_call(
        lay_kernel,
        in_specs=[VMEM] * 4 + [ANYWHERE],
        out_specs=[VMEM] * 2,
        out_shape=[square, square],
        compiler_params=pltpu.CompilerParams(vmem_limit_bytes=8 * 2**20),
        cost_estimate=CHEAP,
        name="laid",
    )(*tokens, after)


def moved(raw, scale, weight, first_moment, second_moment):
    first = first_moment.astype(F32) * (0.9 / FIRST_FIX) + raw * (0.1 * scale / FIRST_FIX)
    second = second_moment.astype(F32) * (0.95 / SECOND_FIX) + (raw * raw) * (
        0.05 * scale * scale / SECOND_FIX
    )
    below = second * lax.rsqrt(second) + 1e-06
    inverse = pl.reciprocal(below, approx=True)
    inverse = inverse * (2.0 - below * inverse)
    return first * inverse + 0.1 * weight.astype(F32)


def folded(values):
    squares = values * values
    total = squares[:8]
    for at in range(8, values.shape[0], 8):
        total = total + squares[at : at + 8]
    out = total[:, :128]
    for at in range(128, values.shape[1], 128):
        out = out + total[:, at : at + 128]
    return out


def moved_rows(raw, scale, w, m, v, out, lanes, base, sums, slot):
    def some(index, total):
        rows = pl.ds(pl.multiple_of(index * ROWS, ROWS), ROWS)
        there = pl.ds(pl.multiple_of(base + index * ROWS, ROWS), ROWS)
        update = moved(raw[rows, lanes], scale, w[there, :], m[rows, :], v[rows, :])
        out[there, lanes] = update.astype(BF)
        return total + folded(update)

    sums[slot] += lax.fori_loop(0, raw.shape[0] // ROWS, some, jnp.zeros((8, 128), F32))


def sums_line(sums):
    lane = lax.broadcasted_iota(jnp.int32, (1, 128), 1)
    line = jnp.zeros((1, 128), F32)
    for slot in range(6):
        line = jnp.where(lane == slot, jnp.sum(sums[slot]), line)
    return line


def down_kernel(cots, full, w, m, v, weight_line, out, line, raw, sums):
    step = pl.program_id(0)

    @pl.when(step == 0)
    def _():
        sums[...] = jnp.zeros_like(sums)

    base = pl.multiple_of(step * 256, 256)
    raw[...] = product_tn(full[:, pl.ds(base, 256)], cots[...])
    moved_rows(raw, HIDDEN_SCALE, w, m, v, out, slice(0, 1024), base, sums, 5)

    @pl.when(step == 1)
    def _():
        line[...] = sums_line(sums) + weight_line[...]


def down_update(cots, full, w, m, v, weight_line):
    block = pl.BlockSpec((256, 1024), lambda i: (i, 0))
    return pl.pallas_call(
        down_kernel,
        grid=(2,),
        in_specs=[VMEM] * 3 + [block] * 2 + [VMEM],
        out_specs=[VMEM] * 2,
        out_shape=[
            jax.ShapeDtypeStruct((512, 1024), BF),
            jax.ShapeDtypeStruct((1, 128), F32),
        ],
        scratch_shapes=[pltpu.VMEM((256, 1024), F32), pltpu.VMEM((6, 8, 128), F32)],
        compiler_params=pltpu.CompilerParams(vmem_limit_bytes=10 * 2**20),
        cost_estimate=CHEAP,
        name="down_update",
    )(cots, full, w, m, v, weight_line)


def wide_kernel(
    turned, full, gate_w, up_w, gate_m, gate_v, up_m, up_v,
    down_line, after, out, lines, raw, sums,
):
    del after
    step = pl.program_id(0)

    @pl.when(step == 0)
    def _():
        sums[...] = jnp.zeros_like(sums)

    base = pl.multiple_of(step * 256, 256)
    raw[...] = product(turned[pl.ds(base, 256), :], full[:, 512:])
    moved_rows(raw, WIDTH_SCALE, gate_w, gate_m, gate_v, out, slice(0, 512), base, sums, 3)
    moved_rows(raw, WIDTH_SCALE, up_w, up_m, up_v, out, slice(512, 1024), base, sums, 4)

    @pl.when(step == 3)
    def _():
        lines[...] = jnp.broadcast_to(sums_line(sums) + down_line[...], lines.shape)


def wide_update(turned, full, gate_w, up_w, moments, down_line, after):
    block = pl.BlockSpec((256, 512), lambda i: (i, 0))
    return pl.pallas_call(
        wide_kernel,
        grid=(4,),
        in_specs=[VMEM] * 4 + [block] * 4 + [VMEM, ANYWHERE],
        out_specs=[VMEM] * 2,
        out_shape=[
            jax.ShapeDtypeStruct((1024, 1024), BF),
            jax.ShapeDtypeStruct((256, 128), F32),
        ],
        scratch_shapes=[pltpu.VMEM((256, 1024), F32), pltpu.VMEM((6, 8, 128), F32)],
        compiler_params=pltpu.CompilerParams(vmem_limit_bytes=10 * 2**20),
        cost_estimate=CHEAP,
        name="wide_update",
    )(turned, full, gate_w, up_w, *moments, down_line, after)


def step_kernel(sums, wide, narrow, gate_out, up_out, down_out):
    step = pl.program_id(0)
    tall = pl.ds(pl.multiple_of(step * 256, 256), 256)
    flat = pl.ds(pl.multiple_of(step * 128, 128), 128)
    totals = jnp.sum(sums[...], axis=0, keepdims=True)

    def ratio(slot):
        return jnp.sqrt(totals[:, slot : slot + 1] / (totals[:, slot + 3 : slot + 4] + 1e-06))

    gate_out[...] = (ratio(0) * wide[tall, :512].astype(F32)).astype(BF)
    up_out[...] = (ratio(1) * wide[tall, 512:].astype(F32)).astype(BF)
    down_out[...] = (ratio(2) * narrow[flat, :].astype(F32)).astype(BF)


def steps(sums, wide, narrow):
    tall = pl.BlockSpec((256, 512), lambda i: (i, 0))
    flat = pl.BlockSpec((128, 1024), lambda i: (i, 0))
    return pl.pallas_call(
        step_kernel,
        grid=(4,),
        in_specs=[VMEM] * 3,
        out_specs=[tall, tall, flat],
        out_shape=[
            jax.ShapeDtypeStruct((1024, 512), BF),
            jax.ShapeDtypeStruct((1024, 512), BF),
            jax.ShapeDtypeStruct((512, 1024), BF),
        ],
        compiler_params=pltpu.CompilerParams(vmem_limit_bytes=8 * 2**20),
        cost_estimate=CHEAP,
        name="steps",
    )(sums, wide, narrow)


def local(
    inputs,
    cotangent,
    gate_weight,
    up_weight,
    down_weight,
    gate_first,
    up_first,
    down_first,
    gate_second,
    up_second,
    down_second,
):
    core = lax.axis_index("row") % 2
    z = lax.axis_index("col")

    both = jnp.stack([inputs, cotangent])
    own = lax.dynamic_slice_in_dim(both, core * 16, 16, axis=1)
    other = lax.dynamic_slice_in_dim(both, (1 - core) * 16, 16, axis=1)
    chip = jnp.concatenate([own, swap(other)], axis=1)
    line = jnp.concatenate(
        [chip, along_first(chip, -1), along_first(chip, 2), along_first(chip, 1)], axis=1
    )
    ahead, behind = along_second(line, -1), along_second(line, 1)
    across = along_second(line, 2)

    *weights, weight_line = staged((gate_weight, up_weight, down_weight))
    mine_a, _ = paired(ahead, behind, weight_line)
    mine_b, _ = paired(line, across, weight_line)
    after = weight_line
    mines = [mine_a, mine_b]
    theirs, pieces = [], []
    for mine in mines:
        theirs.append(swap(mine))
        part, after = first_products(mine, theirs[-1], weights, after)
        sums = col_scatter(part.reshape(8, 64, 1536), z)
        values = local_grads(
            sums[:, :512] * WIDTH_SCALE, sums[:, 512:1024] * WIDTH_SCALE, sums[:, 1024:] * HIDDEN_SCALE
        )
        pieces.append(col_gather(jnp.concatenate(values, axis=1)))
    spot = jnp.reshape(z, (1,)).astype(jnp.int32)
    full, kept_a, given_a = second_products(
        0, spot, pieces[0], weights, (), (pieces[1][3], pieces[1][6])
    )
    got_a = swap(given_a)
    ahead_sum = add(kept_a[:, :128], got_a[:, :128]).astype(BF)
    behind_sum = add(kept_a[:, 128:], got_a[:, 128:]).astype(BF)
    turned, cots = laid((mines[0], theirs[0], mines[1], theirs[1]), behind_sum)
    full, kept_b, given_b = second_products(
        1, spot, pieces[1], weights, (full,), (ahead_sum, turned)
    )
    got_b = swap(given_b)
    narrow, down_line = down_update(cots, full, weights[2], down_first, down_second, weight_line)
    own_sum = add(kept_b[:, :128], got_b[:, :128]).astype(BF)
    across_sum = add(kept_b[:, 128:], got_b[:, 128:]).astype(BF)
    wide, sums = wide_update(
        turned,
        full,
        weights[0],
        weights[1],
        (gate_first, gate_second, up_first, up_second),
        down_line,
        across_sum,
    )
    line_sums = line_total(
        own_sum,
        along_second(ahead_sum, 1),
        along_second(behind_sum, -1),
        along_second(across_sum, 2),
        sums,
    )
    spread = lax.all_to_all(sums, ("row", "col"), 0, 0, tiled=True)
    chip_sum = chip_total(
        line_sums[0],
        along_first(line_sums[1], 1),
        along_first(line_sums[2], 2),
        along_first(line_sums[3], -1),
        spread,
    )
    held, given = chip_sum[:, :16], swap(chip_sum[:, 16:])
    rows = jnp.where(
        core == 0,
        jnp.concatenate([held, given], axis=1),
        jnp.concatenate([given, held], axis=1),
    )
    outputs, input_grad = rows[0] * HIDDEN_SCALE, rows[1] * WIDTH_SCALE

    step_gate, step_up, step_down = steps(spread, wide, narrow)
    return (outputs, input_grad, step_gate, step_up, step_down)


def solution(mesh):
    placed = (
        P("row", "col"),
        P("row", "col"),
        P("col", "row"),
        P("col", "row"),
        P("row", "col"),
        P("col", "row"),
        P("col", "row"),
        P("row", "col"),
        P("col", "row"),
        P("col", "row"),
        P("row", "col"),
    )
    return jax.shard_map(
        local,
        mesh=mesh,
        in_specs=placed,
        out_specs=(
            P("row", "col"),
            P("row", "col"),
            P("col", "row"),
            P("col", "row"),
            P("row", "col"),
        ),
        check_vma=False,
    )
```

```python
import functools
import math

import jax
import jax.numpy as jnp
from jax import lax
from jax.experimental import pallas as pl
from jax.experimental.pallas import tpu as pltpu
from jax.sharding import PartitionSpec as P

D = 8192
FF = 16384
FIRST_FIX = 1.0 - 0.9**20
SECOND_FIX = 1.0 - 0.95**20
BF = jnp.bfloat16
F32 = jnp.float32
ROWS = 32
WIDTH_SCALE = 1.0 / math.sqrt(D)
HIDDEN_SCALE = 1.0 / math.sqrt(FF)
ANYWHERE = pl.BlockSpec(memory_space=pl.ANY)
VMEM = pl.BlockSpec(memory_space=pltpu.VMEM)
CHEAP = pl.CostEstimate(flops=0, bytes_accessed=0, transcendentals=0)


def place(y, x, core):
    return ((y % 4) * 4 + (x % 4)) * 2 + core


CHIPS = [(y, x, core) for y in range(4) for x in range(4) for core in range(2)]
SWAP = [(place(y, x, c), place(y, x, 1 - c)) for y, x, c in CHIPS]


def first_axis(step):
    return [
        (place(y, x, c), place(y, x + step, c) if c == 0 else place(y + step, x, c))
        for y, x, c in CHIPS
    ]


def second_axis(step):
    return [
        (place(y, x, c), place(y + step, x, c) if c == 0 else place(y, x + step, c))
        for y, x, c in CHIPS
    ]


def swap(values):
    return lax.ppermute(values, "row", SWAP)


def along_first(values, step):
    return lax.ppermute(values, "row", first_axis(step))


def along_second(values, step):
    return lax.ppermute(values, "row", second_axis(step))


def along_col(values, step):
    return lax.ppermute(values, "col", [(z, (z + step) % 8) for z in range(8)])


def product(left, right):
    return jnp.dot(left, right, preferred_element_type=F32)


def product_nt(left, right):
    return lax.dot_general(left, right, (((1,), (1,)), ((), ())), preferred_element_type=F32)


def product_tn(left, right):
    return lax.dot_general(left, right, (((0,), (0,)), ((), ())), preferred_element_type=F32)


def add(*terms):
    total = terms[0].astype(F32)
    for term in terms[1:]:
        total = total + term.astype(F32)
    return total


def local_grads(gate_value, up_value, grad_hidden):
    sigmoid_gate = jax.nn.sigmoid(gate_value)
    activated = gate_value * sigmoid_gate
    hidden = (activated * up_value).astype(BF)
    d_up = (grad_hidden * activated).astype(BF)
    d_gate = (
        grad_hidden * up_value * sigmoid_gate * (1.0 + gate_value * (1.0 - sigmoid_gate))
    ).astype(BF)
    return (hidden, d_gate, d_up)


def col_scatter(part, z):
    half = part.shape[1] // 2

    def block(offset):
        return lax.dynamic_index_in_dim(part, (z + offset + 8) % 8, 0, keepdims=False)

    far = block(4)
    down = along_col(far[:half], -1)
    up = along_col(far[half:], 1)
    own_down, own_up = block(-3), block(3)
    down = jnp.concatenate([add(down, own_down[:half]).astype(BF), own_down[half:]], axis=0)
    up = jnp.concatenate([own_up[:half], add(up, own_up[half:]).astype(BF)], axis=0)
    for distance in (2, 1):
        down, up = along_col(down, -1), along_col(up, 1)
        down = add(down, block(-distance)).astype(BF)
        up = add(up, block(distance)).astype(BF)
    down, up = along_col(down, -1), along_col(up, 1)
    return add(block(0), down, up)


def col_gather(own):
    half = own.shape[0] // 2
    low, high = [own], [own]
    for _ in range(3):
        low.append(along_col(low[-1], 1))
        high.append(along_col(high[-1], -1))
    far_low, far_high = along_col(low[-1][:half], 1), along_col(high[-1][half:], -1)
    return (own, high[1], high[2], high[3], far_low, far_high, low[3], low[2], low[1])


def first_kernel(mine, theirs, gate_w, up_w, down_w, after, part, token):
    del after
    token[...] = jnp.zeros_like(token)
    for at, rows in ((0, mine), (256, theirs)):
        part[at : at + 256, :512] = product(rows[0], gate_w[...]).astype(BF)
        part[at : at + 256, 512:1024] = product(rows[0], up_w[...]).astype(BF)
        part[at : at + 256, 1024:] = product_nt(rows[1], down_w[...]).astype(BF)


def first_products(mine, theirs, weights, after):
    return pl.pallas_call(
        first_kernel,
        in_specs=[VMEM] * 5 + [ANYWHERE],
        out_specs=[VMEM] * 2,
        out_shape=[
            jax.ShapeDtypeStruct((512, 1536), BF),
            jax.ShapeDtypeStruct((8, 128), F32),
        ],
        compiler_params=pltpu.CompilerParams(vmem_limit_bytes=8 * 2**20),
        cost_estimate=CHEAP,
        name="first_products",
    )(mine, theirs, *weights, after)


def second_kernel(stream, spot, *refs):
    pieces, (gate_w, up_w, down_w) = refs[:9], refs[9:12]
    full, kept, given = refs[-3:]
    base, row = 512 * stream, 0
    for piece in pieces:
        rows = piece.shape[0]
        block = lax.rem(spot[0] + (row // 64), 8)
        start = pl.multiple_of(base + block * 64 + row % 64, 32)
        full[pl.ds(start, rows), :] = piece[...]
        row += rows
    for at, out in ((base, kept), (base + 256, given)):
        rows = slice(at, at + 256)
        out[0] = product(full[rows, :512], down_w[...]).astype(BF)
        out[1] = (
            product_nt(full[rows, 512:1024], gate_w[...])
            + product_nt(full[rows, 1024:], up_w[...])
        ).astype(BF)


def second_products(stream, spot, pieces, weights, full, after):
    operands = [spot, *pieces, *weights, *full, *after]
    return pl.pallas_call(
        functools.partial(second_kernel, stream),
        in_specs=[pl.BlockSpec(memory_space=pltpu.SMEM)]
        + [VMEM] * (12 + len(full))
        + [ANYWHERE] * len(after),
        out_specs=[VMEM] * 3,
        out_shape=[
            jax.ShapeDtypeStruct((1024, 1536), BF),
            jax.ShapeDtypeStruct((2, 256, 1024), BF),
            jax.ShapeDtypeStruct((2, 256, 1024), BF),
        ],
        input_output_aliases={13: 0} if full else {},
        compiler_params=pltpu.CompilerParams(vmem_limit_bytes=8 * 2**20),
        cost_estimate=CHEAP,
        name="second_products",
    )(*operands)


def sum_kernel(kept, got, first, second):
    first[...] = add(kept[:, :128], got[:, :128]).astype(BF)
    second[...] = add(kept[:, 128:], got[:, 128:]).astype(BF)


def core_sums(kept, got):
    return pl.pallas_call(
        sum_kernel,
        in_specs=[VMEM] * 2,
        out_specs=[VMEM] * 2,
        out_shape=[jax.ShapeDtypeStruct((2, 128, 1024), BF)] * 2,
        compiler_params=pltpu.CompilerParams(vmem_limit_bytes=8 * 2**20),
        cost_estimate=CHEAP,
        name="core_sums",
    )(kept, got)


def line_kernel(own, ahead, behind, across, after, wide, narrow, *outs):
    del after, wide, narrow
    total = add(own[...], ahead[...], behind[...], across[...]).astype(BF)
    for index in range(4):
        outs[index][...] = total[:, 32 * index : 32 * index + 32]


def line_total(own, ahead, behind, across, after, wide, narrow):
    piece = jax.ShapeDtypeStruct((2, 32, 1024), BF)
    return pl.pallas_call(
        line_kernel,
        in_specs=[VMEM] * 4 + [ANYWHERE] + [VMEM] * 2,
        out_specs=[VMEM] * 4,
        out_shape=[piece] * 4,
        compiler_params=pltpu.CompilerParams(vmem_limit_bytes=8 * 2**20),
        cost_estimate=CHEAP,
        name="line_total",
    )(own, ahead, behind, across, after, wide, narrow)


def chip_kernel(own, ahead, across, behind, after, outputs, input_grad):
    del after
    total = add(own[...], ahead[...], across[...], behind[...])
    outputs[...] = total[0] * HIDDEN_SCALE
    input_grad[...] = total[1] * WIDTH_SCALE


def chip_total(own, ahead, across, behind, after):
    return pl.pallas_call(
        chip_kernel,
        in_specs=[VMEM] * 5,
        out_specs=[VMEM] * 2,
        out_shape=[jax.ShapeDtypeStruct((32, 1024), F32)] * 2,
        compiler_params=pltpu.CompilerParams(vmem_limit_bytes=8 * 2**20),
        cost_estimate=CHEAP,
        name="chip_total",
    )(own, ahead, across, behind, after)


def stage_kernel(*refs):
    sources, kept, line, sums = refs[:3], refs[3:6], refs[6], refs[7]
    step = pl.program_id(0)

    @pl.when(step == 0)
    def _():
        sums[...] = jnp.zeros_like(sums)

    for slot in range(3):
        source, target = sources[slot], kept[slot]
        base = step * source.shape[0]

        def some(index, total, source=source, target=target, base=base):
            rows = pl.ds(pl.multiple_of(index * ROWS, ROWS), ROWS)
            values = source[rows, :]
            target[pl.ds(pl.multiple_of(base + index * ROWS, ROWS), ROWS), :] = values
            return total + folded(values.astype(F32))

        sums[slot] += lax.fori_loop(
            0, source.shape[0] // ROWS, some, jnp.zeros((8, 128), F32)
        )

    @pl.when(step == 3)
    def _():
        line[...] = sums_line(sums)


def staged(arrays):
    return pl.pallas_call(
        stage_kernel,
        grid=(4,),
        in_specs=[pl.BlockSpec((a.shape[0] // 4, a.shape[1]), lambda i: (i, 0)) for a in arrays],
        out_specs=[VMEM] * 4,
        out_shape=[jax.ShapeDtypeStruct(a.shape, a.dtype) for a in arrays]
        + [jax.ShapeDtypeStruct((1, 128), F32)],
        scratch_shapes=[pltpu.VMEM((6, 8, 128), F32)],
        compiler_params=pltpu.CompilerParams(vmem_limit_bytes=8 * 2**20),
        cost_estimate=CHEAP,
        name="staged",
    )(*arrays)


def pair_kernel(first, second, after, out, token):
    del after
    token[...] = jnp.zeros_like(token)
    out[:, :128] = first[...]
    out[:, 128:] = second[...]


def paired(first, second, after):
    return pl.pallas_call(
        pair_kernel,
        in_specs=[VMEM] * 2 + [ANYWHERE],
        out_specs=[VMEM] * 2,
        out_shape=[
            jax.ShapeDtypeStruct((2, 256, 1024), BF),
            jax.ShapeDtypeStruct((8, 128), F32),
        ],
        compiler_params=pltpu.CompilerParams(vmem_limit_bytes=8 * 2**20),
        cost_estimate=CHEAP,
        name="paired",
    )(first, second, after)


def lay_kernel(mine_a, theirs_a, mine_b, theirs_b, after, turned, cots):
    del after
    for at, rows in ((0, mine_a), (256, theirs_a), (512, mine_b), (768, theirs_b)):
        turned[:, at : at + 256] = rows[0].T
        cots[at : at + 256, :] = rows[1]


def laid(tokens, after):
    square = jax.ShapeDtypeStruct((1024, 1024), BF)
    return pl.pallas_call(
        lay_kernel,
        in_specs=[VMEM] * 4 + [ANYWHERE],
        out_specs=[VMEM] * 2,
        out_shape=[square, square],
        compiler_params=pltpu.CompilerParams(vmem_limit_bytes=8 * 2**20),
        cost_estimate=CHEAP,
        name="laid",
    )(*tokens, after)


def moved(raw, scale, weight, first_moment, second_moment):
    first = first_moment.astype(F32) * (0.9 / FIRST_FIX) + raw * (0.1 * scale / FIRST_FIX)
    second = second_moment.astype(F32) * (0.95 / SECOND_FIX) + (raw * raw) * (
        0.05 * scale * scale / SECOND_FIX
    )
    below = second * lax.rsqrt(second) + 1e-06
    inverse = pl.reciprocal(below, approx=True)
    inverse = inverse * (2.0 - below * inverse)
    return first * inverse + 0.1 * weight.astype(F32)


def folded(values):
    squares = values * values
    total = squares[:8]
    for at in range(8, values.shape[0], 8):
        total = total + squares[at : at + 8]
    out = total[:, :128]
    for at in range(128, values.shape[1], 128):
        out = out + total[:, at : at + 128]
    return out


def moved_rows(raw, scale, w, m, v, out, lanes, base, sums, slot):
    def some(index, total):
        rows = pl.ds(pl.multiple_of(index * ROWS, ROWS), ROWS)
        there = pl.ds(pl.multiple_of(base + index * ROWS, ROWS), ROWS)
        update = moved(raw[rows, lanes], scale, w[there, :], m[rows, :], v[rows, :])
        out[there, lanes] = update.astype(BF)
        return total + folded(update)

    sums[slot] += lax.fori_loop(0, raw.shape[0] // ROWS, some, jnp.zeros((8, 128), F32))


def sums_line(sums):
    lane = lax.broadcasted_iota(jnp.int32, (1, 128), 1)
    line = jnp.zeros((1, 128), F32)
    for slot in range(6):
        line = jnp.where(lane == slot, jnp.sum(sums[slot]), line)
    return line


def down_kernel(cots, full, w, m, v, weight_line, out, line, raw, sums):
    step = pl.program_id(0)

    @pl.when(step == 0)
    def _():
        sums[...] = jnp.zeros_like(sums)

    base = pl.multiple_of(step * 256, 256)
    raw[...] = product_tn(full[:, pl.ds(base, 256)], cots[...])
    moved_rows(raw, HIDDEN_SCALE, w, m, v, out, slice(0, 1024), base, sums, 5)

    @pl.when(step == 1)
    def _():
        line[...] = sums_line(sums) + weight_line[...]


def down_update(cots, full, w, m, v, weight_line):
    block = pl.BlockSpec((256, 1024), lambda i: (i, 0))
    return pl.pallas_call(
        down_kernel,
        grid=(2,),
        in_specs=[VMEM] * 3 + [block] * 2 + [VMEM],
        out_specs=[VMEM] * 2,
        out_shape=[
            jax.ShapeDtypeStruct((512, 1024), BF),
            jax.ShapeDtypeStruct((1, 128), F32),
        ],
        scratch_shapes=[pltpu.VMEM((256, 1024), F32), pltpu.VMEM((6, 8, 128), F32)],
        compiler_params=pltpu.CompilerParams(vmem_limit_bytes=10 * 2**20),
        cost_estimate=CHEAP,
        name="down_update",
    )(cots, full, w, m, v, weight_line)


def wide_kernel(
    turned, full, gate_w, up_w, gate_m, gate_v, up_m, up_v,
    down_line, after, out, lines, raw, sums,
):
    del after
    step = pl.program_id(0)

    @pl.when(step == 0)
    def _():
        sums[...] = jnp.zeros_like(sums)

    base = pl.multiple_of(step * 256, 256)
    raw[...] = product(turned[pl.ds(base, 256), :], full[:, 512:])
    moved_rows(raw, WIDTH_SCALE, gate_w, gate_m, gate_v, out, slice(0, 512), base, sums, 3)
    moved_rows(raw, WIDTH_SCALE, up_w, up_m, up_v, out, slice(512, 1024), base, sums, 4)

    @pl.when(step == 3)
    def _():
        lines[...] = jnp.broadcast_to(sums_line(sums) + down_line[...], lines.shape)


def wide_update(turned, full, gate_w, up_w, moments, down_line, after):
    block = pl.BlockSpec((256, 512), lambda i: (i, 0))
    return pl.pallas_call(
        wide_kernel,
        grid=(4,),
        in_specs=[VMEM] * 4 + [block] * 4 + [VMEM, ANYWHERE],
        out_specs=[VMEM] * 2,
        out_shape=[
            jax.ShapeDtypeStruct((1024, 1024), BF),
            jax.ShapeDtypeStruct((256, 128), F32),
        ],
        scratch_shapes=[pltpu.VMEM((256, 1024), F32), pltpu.VMEM((6, 8, 128), F32)],
        compiler_params=pltpu.CompilerParams(vmem_limit_bytes=10 * 2**20),
        cost_estimate=CHEAP,
        name="wide_update",
    )(turned, full, gate_w, up_w, *moments, down_line, after)


def step_kernel(sums, wide, narrow, gate_out, up_out, down_out):
    step = pl.program_id(0)
    tall = pl.ds(pl.multiple_of(step * 256, 256), 256)
    flat = pl.ds(pl.multiple_of(step * 128, 128), 128)
    totals = jnp.sum(sums[...], axis=0, keepdims=True)

    def ratio(slot):
        return jnp.sqrt(totals[:, slot : slot + 1] / (totals[:, slot + 3 : slot + 4] + 1e-06))

    gate_out[...] = (ratio(0) * wide[tall, :512].astype(F32)).astype(BF)
    up_out[...] = (ratio(1) * wide[tall, 512:].astype(F32)).astype(BF)
    down_out[...] = (ratio(2) * narrow[flat, :].astype(F32)).astype(BF)


def steps(sums, wide, narrow):
    tall = pl.BlockSpec((256, 512), lambda i: (i, 0))
    flat = pl.BlockSpec((128, 1024), lambda i: (i, 0))
    return pl.pallas_call(
        step_kernel,
        grid=(4,),
        in_specs=[VMEM] * 3,
        out_specs=[tall, tall, flat],
        out_shape=[
            jax.ShapeDtypeStruct((1024, 512), BF),
            jax.ShapeDtypeStruct((1024, 512), BF),
            jax.ShapeDtypeStruct((512, 1024), BF),
        ],
        compiler_params=pltpu.CompilerParams(vmem_limit_bytes=8 * 2**20),
        cost_estimate=CHEAP,
        name="steps",
    )(sums, wide, narrow)


def local(
    inputs,
    cotangent,
    gate_weight,
    up_weight,
    down_weight,
    gate_first,
    up_first,
    down_first,
    gate_second,
    up_second,
    down_second,
):
    z = lax.axis_index("col")

    chip = jnp.stack([inputs, cotangent])
    line = jnp.concatenate(
        [chip, along_first(chip, -1), along_first(chip, 2), along_first(chip, 1)], axis=1
    )
    ahead, behind = along_second(line, -1), along_second(line, 1)
    across = along_second(line, 2)

    *weights, weight_line = staged((gate_weight, up_weight, down_weight))
    mine_a, _ = paired(ahead, behind, weight_line)
    mine_b, _ = paired(line, across, weight_line)
    after = weight_line
    mines = [mine_a, mine_b]
    theirs, pieces = [], []
    for mine in mines:
        theirs.append(swap(mine))
        part, after = first_products(mine, theirs[-1], weights, after)
        sums = col_scatter(part.reshape(8, 64, 1536), z)
        values = local_grads(
            sums[:, :512] * WIDTH_SCALE, sums[:, 512:1024] * WIDTH_SCALE, sums[:, 1024:] * HIDDEN_SCALE
        )
        pieces.append(col_gather(jnp.concatenate(values, axis=1)))
    spot = jnp.reshape(z, (1,)).astype(jnp.int32)
    full, kept_a, given_a = second_products(
        0, spot, pieces[0], weights, (), (pieces[1][3], pieces[1][6])
    )
    ahead_sum, behind_sum = core_sums(kept_a, swap(given_a))
    turned, cots = laid((mines[0], theirs[0], mines[1], theirs[1]), behind_sum)
    full, kept_b, given_b = second_products(
        1, spot, pieces[1], weights, (full,), (ahead_sum, turned)
    )
    own_sum, across_sum = core_sums(kept_b, swap(given_b))
    narrow, down_line = down_update(cots, full, weights[2], down_first, down_second, weight_line)
    wide, sums = wide_update(
        turned,
        full,
        weights[0],
        weights[1],
        (gate_first, gate_second, up_first, up_second),
        down_line,
        across_sum,
    )
    line_sums = line_total(
        own_sum,
        along_second(ahead_sum, 1),
        along_second(behind_sum, -1),
        along_second(across_sum, 2),
        sums,
        wide,
        narrow,
    )
    spread = lax.all_to_all(sums, ("row", "col"), 0, 0, tiled=True)
    outputs, input_grad = chip_total(
        line_sums[0],
        along_first(line_sums[1], 1),
        along_first(line_sums[2], 2),
        along_first(line_sums[3], -1),
        spread,
    )
    step_gate, step_up, step_down = steps(spread, wide, narrow)
    return (outputs, input_grad, step_gate, step_up, step_down)


def solution(mesh):
    placed = (
        P("row", "col"),
        P("row", "col"),
        P("col", "row"),
        P("col", "row"),
        P("row", "col"),
        P("col", "row"),
        P("col", "row"),
        P("row", "col"),
        P("col", "row"),
        P("col", "row"),
        P("row", "col"),
    )
    return jax.shard_map(
        local,
        mesh=mesh,
        in_specs=placed,
        out_specs=(
            P("row", "col"),
            P("row", "col"),
            P("col", "row"),
            P("col", "row"),
            P("row", "col"),
        ),
        check_vma=False,
    )
```

```python
import functools
import math

import jax
import jax.numpy as jnp
from jax import lax
from jax.experimental import pallas as pl
from jax.experimental.pallas import tpu as pltpu
from jax.sharding import PartitionSpec as P

D = 8192
FF = 16384
FIRST_FIX = 1.0 - 0.9**20
SECOND_FIX = 1.0 - 0.95**20
BF = jnp.bfloat16
F32 = jnp.float32
ROWS = 64
WIDTH_SCALE = 1.0 / math.sqrt(D)
HIDDEN_SCALE = 1.0 / math.sqrt(FF)
ANYWHERE = pl.BlockSpec(memory_space=pl.ANY)
VMEM = pl.BlockSpec(memory_space=pltpu.VMEM)
CHEAP = pl.CostEstimate(flops=0, bytes_accessed=0, transcendentals=0)


def place(y, x, core):
    return ((y % 4) * 4 + (x % 4)) * 2 + core


CHIPS = [(y, x, core) for y in range(4) for x in range(4) for core in range(2)]
SWAP = [(place(y, x, c), place(y, x, 1 - c)) for y, x, c in CHIPS]


def first_axis(step):
    return [
        (place(y, x, c), place(y, x + step, c) if c == 0 else place(y + step, x, c))
        for y, x, c in CHIPS
    ]


def second_axis(step):
    return [
        (place(y, x, c), place(y + step, x, c) if c == 0 else place(y, x + step, c))
        for y, x, c in CHIPS
    ]


def swap(values):
    return lax.ppermute(values, "row", SWAP)


def along_first(values, step):
    return lax.ppermute(values, "row", first_axis(step))


def along_second(values, step):
    return lax.ppermute(values, "row", second_axis(step))


def along_col(values, step):
    return lax.ppermute(values, "col", [(z, (z + step) % 8) for z in range(8)])


def product(left, right):
    return jnp.dot(left, right, preferred_element_type=F32)


def product_nt(left, right):
    return lax.dot_general(left, right, (((1,), (1,)), ((), ())), preferred_element_type=F32)


def product_tn(left, right):
    return lax.dot_general(left, right, (((0,), (0,)), ((), ())), preferred_element_type=F32)


def add(*terms):
    total = terms[0].astype(F32)
    for term in terms[1:]:
        total = total + term.astype(F32)
    return total


def local_grads(gate_value, up_value, grad_hidden):
    sigmoid_gate = jax.nn.sigmoid(gate_value)
    activated = gate_value * sigmoid_gate
    hidden = (activated * up_value).astype(BF)
    d_up = (grad_hidden * activated).astype(BF)
    d_gate = (
        grad_hidden * up_value * sigmoid_gate * (1.0 + gate_value * (1.0 - sigmoid_gate))
    ).astype(BF)
    return (hidden, d_gate, d_up)


def col_scatter(part, z):
    half = part.shape[1] // 2

    def block(offset):
        return lax.dynamic_index_in_dim(part, (z + offset + 8) % 8, 0, keepdims=False)

    far = block(4)
    down = along_col(far[:half], -1)
    up = along_col(far[half:], 1)
    own_down, own_up = block(-3), block(3)
    down = jnp.concatenate([add(down, own_down[:half]).astype(BF), own_down[half:]], axis=0)
    up = jnp.concatenate([own_up[:half], add(up, own_up[half:]).astype(BF)], axis=0)
    for distance in (2, 1):
        down, up = along_col(down, -1), along_col(up, 1)
        down = add(down, block(-distance)).astype(BF)
        up = add(up, block(distance)).astype(BF)
    down, up = along_col(down, -1), along_col(up, 1)
    return add(block(0), down, up)


def col_gather(own):
    half = own.shape[0] // 2
    low, high = [own], [own]
    for _ in range(3):
        low.append(along_col(low[-1], 1))
        high.append(along_col(high[-1], -1))
    far_low, far_high = along_col(low[-1][:half], 1), along_col(high[-1][half:], -1)
    return (own, high[1], high[2], high[3], far_low, far_high, low[3], low[2], low[1])


def first_kernel(at, rows, gate_w, up_w, down_w, after, *refs):
    del after
    part, token = refs[-2:]
    token[...] = jnp.zeros_like(token)
    part[at : at + 256, :512] = product(rows[0], gate_w[...]).astype(BF)
    part[at : at + 256, 512:1024] = product(rows[0], up_w[...]).astype(BF)
    part[at : at + 256, 1024:] = product_nt(rows[1], down_w[...]).astype(BF)


def first_products(at, rows, weights, after, part):
    return pl.pallas_call(
        functools.partial(first_kernel, at),
        in_specs=[VMEM] * 4 + [ANYWHERE] + [VMEM] * len(part),
        out_specs=[VMEM] * 2,
        out_shape=[
            jax.ShapeDtypeStruct((512, 1536), BF),
            jax.ShapeDtypeStruct((8, 128), F32),
        ],
        input_output_aliases={5: 0} if part else {},
        compiler_params=pltpu.CompilerParams(vmem_limit_bytes=8 * 2**20),
        cost_estimate=CHEAP,
        name="first_products",
    )(rows, *weights, after, *part)


def second_kernel(stream, spot, *refs):
    pieces, (gate_w, up_w, down_w) = refs[:9], refs[9:12]
    full, kept, given = refs[-3:]
    base, row = 512 * stream, 0
    for piece in pieces:
        rows = piece.shape[0]
        block = lax.rem(spot[0] + (row // 64), 8)
        start = pl.multiple_of(base + block * 64 + row % 64, 32)
        full[pl.ds(start, rows), :] = piece[...]
        row += rows
    for at, out in ((base, kept), (base + 256, given)):
        rows = slice(at, at + 256)
        out[0] = product(full[rows, :512], down_w[...]).astype(BF)
        out[1] = (
            product_nt(full[rows, 512:1024], gate_w[...])
            + product_nt(full[rows, 1024:], up_w[...])
        ).astype(BF)


def second_products(stream, spot, pieces, weights, full, after):
    operands = [spot, *pieces, *weights, *full, *after]
    return pl.pallas_call(
        functools.partial(second_kernel, stream),
        in_specs=[pl.BlockSpec(memory_space=pltpu.SMEM)]
        + [VMEM] * (12 + len(full))
        + [ANYWHERE] * len(after),
        out_specs=[VMEM] * 3,
        out_shape=[
            jax.ShapeDtypeStruct((1024, 1536), BF),
            jax.ShapeDtypeStruct((2, 256, 1024), BF),
            jax.ShapeDtypeStruct((2, 256, 1024), BF),
        ],
        input_output_aliases={13: 0} if full else {},
        compiler_params=pltpu.CompilerParams(vmem_limit_bytes=8 * 2**20),
        cost_estimate=CHEAP,
        name="second_products",
    )(*operands)


def sum_kernel(kept, got, first, second):
    first[...] = add(kept[:, :128], got[:, :128]).astype(BF)
    second[...] = add(kept[:, 128:], got[:, 128:]).astype(BF)


def core_sums(kept, got):
    return pl.pallas_call(
        sum_kernel,
        in_specs=[VMEM] * 2,
        out_specs=[VMEM] * 2,
        out_shape=[jax.ShapeDtypeStruct((2, 128, 1024), BF)] * 2,
        compiler_params=pltpu.CompilerParams(vmem_limit_bytes=8 * 2**20),
        cost_estimate=CHEAP,
        name="core_sums",
    )(kept, got)


def line_kernel(own, ahead, behind, across, after, wide, narrow, *outs):
    del after, wide, narrow
    total = add(own[...], ahead[...], behind[...], across[...]).astype(BF)
    for index in range(4):
        outs[index][...] = total[:, 32 * index : 32 * index + 32]


def line_total(own, ahead, behind, across, after, wide, narrow):
    piece = jax.ShapeDtypeStruct((2, 32, 1024), BF)
    return pl.pallas_call(
        line_kernel,
        in_specs=[VMEM] * 4 + [ANYWHERE] + [VMEM] * 2,
        out_specs=[VMEM] * 4,
        out_shape=[piece] * 4,
        compiler_params=pltpu.CompilerParams(vmem_limit_bytes=8 * 2**20),
        cost_estimate=CHEAP,
        name="line_total",
    )(own, ahead, behind, across, after, wide, narrow)


def chip_kernel(own, ahead, across, behind, after, outputs, input_grad):
    del after
    total = add(own[...], ahead[...], across[...], behind[...])
    outputs[...] = total[0] * HIDDEN_SCALE
    input_grad[...] = total[1] * WIDTH_SCALE


def chip_total(own, ahead, across, behind, after):
    return pl.pallas_call(
        chip_kernel,
        in_specs=[VMEM] * 5,
        out_specs=[VMEM] * 2,
        out_shape=[jax.ShapeDtypeStruct((32, 1024), F32)] * 2,
        compiler_params=pltpu.CompilerParams(vmem_limit_bytes=8 * 2**20),
        cost_estimate=CHEAP,
        name="chip_total",
    )(own, ahead, across, behind, after)


def stage_kernel(*refs):
    sources, kept, line, sums = refs[:3], refs[3:6], refs[6], refs[7]
    step = pl.program_id(0)

    @pl.when(step == 0)
    def _():
        sums[...] = jnp.zeros_like(sums)

    for slot in range(3):
        source, target = sources[slot], kept[slot]
        base = step * source.shape[0]

        def some(index, total, source=source, target=target, base=base):
            rows = pl.ds(pl.multiple_of(index * ROWS, ROWS), ROWS)
            values = source[rows, :]
            target[pl.ds(pl.multiple_of(base + index * ROWS, ROWS), ROWS), :] = values
            return total + folded(values.astype(F32))

        sums[slot] += lax.fori_loop(
            0, source.shape[0] // ROWS, some, jnp.zeros((8, 128), F32)
        )

    @pl.when(step == 3)
    def _():
        line[...] = sums_line(sums)


def staged(arrays):
    return pl.pallas_call(
        stage_kernel,
        grid=(4,),
        in_specs=[pl.BlockSpec((a.shape[0] // 4, a.shape[1]), lambda i: (i, 0)) for a in arrays],
        out_specs=[VMEM] * 4,
        out_shape=[jax.ShapeDtypeStruct(a.shape, a.dtype) for a in arrays]
        + [jax.ShapeDtypeStruct((1, 128), F32)],
        scratch_shapes=[pltpu.VMEM((6, 8, 128), F32)],
        compiler_params=pltpu.CompilerParams(vmem_limit_bytes=8 * 2**20),
        cost_estimate=CHEAP,
        name="staged",
    )(*arrays)


def pair_kernel(first, second, after, out, token):
    del after
    token[...] = jnp.zeros_like(token)
    out[:, :128] = first[...]
    out[:, 128:] = second[...]


def paired(first, second, after):
    return pl.pallas_call(
        pair_kernel,
        in_specs=[VMEM] * 2 + [ANYWHERE],
        out_specs=[VMEM] * 2,
        out_shape=[
            jax.ShapeDtypeStruct((2, 256, 1024), BF),
            jax.ShapeDtypeStruct((8, 128), F32),
        ],
        compiler_params=pltpu.CompilerParams(vmem_limit_bytes=8 * 2**20),
        cost_estimate=CHEAP,
        name="paired",
    )(first, second, after)


def lay_kernel(mine_a, theirs_a, mine_b, theirs_b, after, turned, cots):
    del after
    for at, rows in ((0, mine_a), (256, theirs_a), (512, mine_b), (768, theirs_b)):
        turned[:, at : at + 256] = rows[0].T
        cots[at : at + 256, :] = rows[1]


def laid(tokens, after):
    square = jax.ShapeDtypeStruct((1024, 1024), BF)
    return pl.pallas_call(
        lay_kernel,
        in_specs=[VMEM] * 4 + [ANYWHERE],
        out_specs=[VMEM] * 2,
        out_shape=[square, square],
        compiler_params=pltpu.CompilerParams(vmem_limit_bytes=8 * 2**20),
        cost_estimate=CHEAP,
        name="laid",
    )(*tokens, after)


def moved(raw, scale, weight, first_moment, second_moment):
    first = first_moment.astype(F32) * (0.9 / FIRST_FIX) + raw * (0.1 * scale / FIRST_FIX)
    second = second_moment.astype(F32) * (0.95 / SECOND_FIX) + (raw * raw) * (
        0.05 * scale * scale / SECOND_FIX
    )
    below = second * lax.rsqrt(second) + 1e-06
    inverse = pl.reciprocal(below, approx=True)
    inverse = inverse * (2.0 - below * inverse)
    return first * inverse + 0.1 * weight.astype(F32)


def folded(values):
    squares = values * values
    total = squares[:8]
    for at in range(8, values.shape[0], 8):
        total = total + squares[at : at + 8]
    out = total[:, :128]
    for at in range(128, values.shape[1], 128):
        out = out + total[:, at : at + 128]
    return out


def moved_rows(raw, scale, w, m, v, out, lanes, base, sums, slot):
    def some(index, total):
        rows = pl.ds(pl.multiple_of(index * ROWS, ROWS), ROWS)
        there = pl.ds(pl.multiple_of(base + index * ROWS, ROWS), ROWS)
        update = moved(raw[rows, lanes], scale, w[there, :], m[rows, :], v[rows, :])
        out[there, lanes] = update.astype(BF)
        return total + folded(update)

    sums[slot] += lax.fori_loop(0, raw.shape[0] // ROWS, some, jnp.zeros((8, 128), F32))


def sums_line(sums):
    lane = lax.broadcasted_iota(jnp.int32, (1, 128), 1)
    line = jnp.zeros((1, 128), F32)
    for slot in range(6):
        line = jnp.where(lane == slot, jnp.sum(sums[slot]), line)
    return line


def down_kernel(cots, full, w, m, v, weight_line, out, line, raw, sums):
    step = pl.program_id(0)

    @pl.when(step == 0)
    def _():
        sums[...] = jnp.zeros_like(sums)

    base = pl.multiple_of(step * 256, 256)
    raw[...] = product_tn(full[:, pl.ds(base, 256)], cots[...])
    moved_rows(raw, HIDDEN_SCALE, w, m, v, out, slice(0, 1024), base, sums, 5)

    @pl.when(step == 1)
    def _():
        line[...] = sums_line(sums) + weight_line[...]


def down_update(cots, full, w, m, v, weight_line):
    block = pl.BlockSpec((256, 1024), lambda i: (i, 0))
    return pl.pallas_call(
        down_kernel,
        grid=(2,),
        in_specs=[VMEM] * 3 + [block] * 2 + [VMEM],
        out_specs=[VMEM] * 2,
        out_shape=[
            jax.ShapeDtypeStruct((512, 1024), BF),
            jax.ShapeDtypeStruct((1, 128), F32),
        ],
        scratch_shapes=[pltpu.VMEM((256, 1024), F32), pltpu.VMEM((6, 8, 128), F32)],
        compiler_params=pltpu.CompilerParams(vmem_limit_bytes=10 * 2**20),
        cost_estimate=CHEAP,
        name="down_update",
    )(cots, full, w, m, v, weight_line)


def wide_kernel(
    turned, full, gate_w, up_w, gate_m, gate_v, up_m, up_v,
    down_line, after, out, lines, raw, sums,
):
    del after
    step = pl.program_id(0)

    @pl.when(step == 0)
    def _():
        sums[...] = jnp.zeros_like(sums)

    base = pl.multiple_of(step * 256, 256)
    raw[...] = product(turned[pl.ds(base, 256), :], full[:, 512:])
    moved_rows(raw, WIDTH_SCALE, gate_w, gate_m, gate_v, out, slice(0, 512), base, sums, 3)
    moved_rows(raw, WIDTH_SCALE, up_w, up_m, up_v, out, slice(512, 1024), base, sums, 4)

    @pl.when(step == 3)
    def _():
        lines[...] = jnp.broadcast_to(sums_line(sums) + down_line[...], lines.shape)


def wide_update(turned, full, gate_w, up_w, moments, down_line, after):
    block = pl.BlockSpec((256, 512), lambda i: (i, 0))
    return pl.pallas_call(
        wide_kernel,
        grid=(4,),
        in_specs=[VMEM] * 4 + [block] * 4 + [VMEM, ANYWHERE],
        out_specs=[VMEM] * 2,
        out_shape=[
            jax.ShapeDtypeStruct((1024, 1024), BF),
            jax.ShapeDtypeStruct((256, 128), F32),
        ],
        scratch_shapes=[pltpu.VMEM((256, 1024), F32), pltpu.VMEM((6, 8, 128), F32)],
        compiler_params=pltpu.CompilerParams(vmem_limit_bytes=10 * 2**20),
        cost_estimate=CHEAP,
        name="wide_update",
    )(turned, full, gate_w, up_w, *moments, down_line, after)


def step_kernel(sums, wide, narrow, gate_out, up_out, down_out):
    step = pl.program_id(0)
    tall = pl.ds(pl.multiple_of(step * 256, 256), 256)
    flat = pl.ds(pl.multiple_of(step * 128, 128), 128)
    totals = jnp.sum(sums[...], axis=0, keepdims=True)

    def ratio(slot):
        return jnp.sqrt(totals[:, slot : slot + 1] / (totals[:, slot + 3 : slot + 4] + 1e-06))

    gate_out[...] = (ratio(0) * wide[tall, :512].astype(F32)).astype(BF)
    up_out[...] = (ratio(1) * wide[tall, 512:].astype(F32)).astype(BF)
    down_out[...] = (ratio(2) * narrow[flat, :].astype(F32)).astype(BF)


def steps(sums, wide, narrow):
    tall = pl.BlockSpec((256, 512), lambda i: (i, 0))
    flat = pl.BlockSpec((128, 1024), lambda i: (i, 0))
    return pl.pallas_call(
        step_kernel,
        grid=(4,),
        in_specs=[VMEM] * 3,
        out_specs=[tall, tall, flat],
        out_shape=[
            jax.ShapeDtypeStruct((1024, 512), BF),
            jax.ShapeDtypeStruct((1024, 512), BF),
            jax.ShapeDtypeStruct((512, 1024), BF),
        ],
        compiler_params=pltpu.CompilerParams(vmem_limit_bytes=8 * 2**20),
        cost_estimate=CHEAP,
        name="steps",
    )(sums, wide, narrow)


def local(
    inputs,
    cotangent,
    gate_weight,
    up_weight,
    down_weight,
    gate_first,
    up_first,
    down_first,
    gate_second,
    up_second,
    down_second,
):
    z = lax.axis_index("col")

    chip = jnp.stack([inputs, cotangent])
    line = jnp.concatenate(
        [chip, along_first(chip, -1), along_first(chip, 2), along_first(chip, 1)], axis=1
    )
    ahead, behind = along_second(line, -1), along_second(line, 1)
    across = along_second(line, 2)

    *weights, weight_line = staged((gate_weight, up_weight, down_weight))
    mine_a, _ = paired(ahead, behind, weight_line)
    mine_b, _ = paired(line, across, weight_line)
    after = weight_line
    mines = [mine_a, mine_b]
    theirs, pieces = [], []
    for mine in mines:
        theirs.append(swap(mine))
        part, after = first_products(0, mine, weights, after, ())
        part, after = first_products(256, theirs[-1], weights, after, (part,))
        sums = col_scatter(part.reshape(8, 64, 1536), z)
        values = local_grads(
            sums[:, :512] * WIDTH_SCALE, sums[:, 512:1024] * WIDTH_SCALE, sums[:, 1024:] * HIDDEN_SCALE
        )
        pieces.append(col_gather(jnp.concatenate(values, axis=1)))
    spot = jnp.reshape(z, (1,)).astype(jnp.int32)
    full, kept_a, given_a = second_products(
        0, spot, pieces[0], weights, (), (pieces[1][3], pieces[1][6])
    )
    ahead_sum, behind_sum = core_sums(kept_a, swap(given_a))
    turned, cots = laid((mines[0], theirs[0], mines[1], theirs[1]), behind_sum)
    full, kept_b, given_b = second_products(
        1, spot, pieces[1], weights, (full,), (ahead_sum, turned)
    )
    own_sum, across_sum = core_sums(kept_b, swap(given_b))
    narrow, down_line = down_update(cots, full, weights[2], down_first, down_second, weight_line)
    wide, sums = wide_update(
        turned,
        full,
        weights[0],
        weights[1],
        (gate_first, gate_second, up_first, up_second),
        down_line,
        across_sum,
    )
    line_sums = line_total(
        own_sum,
        along_second(ahead_sum, 1),
        along_second(behind_sum, -1),
        along_second(across_sum, 2),
        sums,
        wide,
        narrow,
    )
    spread = lax.all_to_all(sums, ("row", "col"), 0, 0, tiled=True)
    outputs, input_grad = chip_total(
        line_sums[0],
        along_first(line_sums[1], 1),
        along_first(line_sums[2], 2),
        along_first(line_sums[3], -1),
        spread,
    )
    step_gate, step_up, step_down = steps(spread, wide, narrow)
    return (outputs, input_grad, step_gate, step_up, step_down)


def solution(mesh):
    placed = (
        P("row", "col"),
        P("row", "col"),
        P("col", "row"),
        P("col", "row"),
        P("row", "col"),
        P("col", "row"),
        P("col", "row"),
        P("row", "col"),
        P("col", "row"),
        P("col", "row"),
        P("row", "col"),
    )
    return jax.shard_map(
        local,
        mesh=mesh,
        in_specs=placed,
        out_specs=(
            P("row", "col"),
            P("row", "col"),
            P("col", "row"),
            P("col", "row"),
            P("row", "col"),
        ),
        check_vma=False,
    )
```

```python
import functools
import math

import jax
import jax.numpy as jnp
from jax import lax
from jax.experimental import pallas as pl
from jax.experimental.pallas import tpu as pltpu
from jax.sharding import PartitionSpec as P

D = 8192
FF = 16384
FIRST_FIX = 1.0 - 0.9**20
SECOND_FIX = 1.0 - 0.95**20
BF = jnp.bfloat16
F32 = jnp.float32
ROWS = 64
WIDTH_SCALE = 1.0 / math.sqrt(D)
HIDDEN_SCALE = 1.0 / math.sqrt(FF)
ANYWHERE = pl.BlockSpec(memory_space=pl.ANY)
VMEM = pl.BlockSpec(memory_space=pltpu.VMEM)
CHEAP = pl.CostEstimate(flops=0, bytes_accessed=0, transcendentals=0)


def place(y, x, core):
    return ((y % 4) * 4 + (x % 4)) * 2 + core


CHIPS = [(y, x, core) for y in range(4) for x in range(4) for core in range(2)]
SWAP = [(place(y, x, c), place(y, x, 1 - c)) for y, x, c in CHIPS]


def first_axis(step):
    return [
        (place(y, x, c), place(y, x + step, c) if c == 0 else place(y + step, x, c))
        for y, x, c in CHIPS
    ]


def second_axis(step):
    return [
        (place(y, x, c), place(y + step, x, c) if c == 0 else place(y, x + step, c))
        for y, x, c in CHIPS
    ]


def swap(values):
    return lax.ppermute(values, "row", SWAP)


def along_first(values, step):
    return lax.ppermute(values, "row", first_axis(step))


def along_second(values, step):
    return lax.ppermute(values, "row", second_axis(step))


def along_col(values, step):
    return lax.ppermute(values, "col", [(z, (z + step) % 8) for z in range(8)])


def product(left, right):
    return jnp.dot(left, right, preferred_element_type=F32)


def product_nt(left, right):
    return lax.dot_general(left, right, (((1,), (1,)), ((), ())), preferred_element_type=F32)


def product_tn(left, right):
    return lax.dot_general(left, right, (((0,), (0,)), ((), ())), preferred_element_type=F32)


def add(*terms):
    total = terms[0].astype(F32)
    for term in terms[1:]:
        total = total + term.astype(F32)
    return total


def local_grads(gate_value, up_value, grad_hidden):
    sigmoid_gate = jax.nn.sigmoid(gate_value)
    activated = gate_value * sigmoid_gate
    hidden = (activated * up_value).astype(BF)
    d_up = (grad_hidden * activated).astype(BF)
    d_gate = (
        grad_hidden * up_value * sigmoid_gate * (1.0 + gate_value * (1.0 - sigmoid_gate))
    ).astype(BF)
    return (hidden, d_gate, d_up)


def col_scatter(part, z):
    half = part.shape[1] // 2

    def block(offset):
        return lax.dynamic_index_in_dim(part, (z + offset + 8) % 8, 0, keepdims=False)

    far = block(4)
    down = along_col(far[:half], -1)
    up = along_col(far[half:], 1)
    own_down, own_up = block(-3), block(3)
    down = jnp.concatenate([add(down, own_down[:half]).astype(BF), own_down[half:]], axis=0)
    up = jnp.concatenate([own_up[:half], add(up, own_up[half:]).astype(BF)], axis=0)
    for distance in (2, 1):
        down, up = along_col(down, -1), along_col(up, 1)
        down = add(down, block(-distance)).astype(BF)
        up = add(up, block(distance)).astype(BF)
    down, up = along_col(down, -1), along_col(up, 1)
    return block(0), down, up


def col_gather(own):
    half = own.shape[0] // 2
    low, high = [own], [own]
    for _ in range(3):
        low.append(along_col(low[-1], 1))
        high.append(along_col(high[-1], -1))
    far_low, far_high = along_col(low[-1][:half], 1), along_col(high[-1][half:], -1)
    return (own, high[1], high[2], high[3], far_low, far_high, low[3], low[2], low[1])


def value_kernel(own, down, up, out):
    sums = [
        add(own[:, lanes], down[:, lanes], up[:, lanes])
        for lanes in (slice(0, 512), slice(512, 1024), slice(1024, 1536))
    ]
    values = local_grads(sums[0] * WIDTH_SCALE, sums[1] * WIDTH_SCALE, sums[2] * HIDDEN_SCALE)
    for index, value in enumerate(values):
        out[:, 512 * index : 512 * index + 512] = value


def unit_values(own, down, up):
    return pl.pallas_call(
        value_kernel,
        in_specs=[VMEM] * 3,
        out_specs=VMEM,
        out_shape=jax.ShapeDtypeStruct(own.shape, BF),
        compiler_params=pltpu.CompilerParams(vmem_limit_bytes=8 * 2**20),
        cost_estimate=CHEAP,
        name="unit_values",
    )(own, down, up)


def first_kernel(mine, theirs, gate_w, up_w, down_w, after, part, token):
    del after
    token[...] = jnp.zeros_like(token)
    for at, rows in ((0, mine), (256, theirs)):
        part[at : at + 256, :512] = product(rows[0], gate_w[...]).astype(BF)
        part[at : at + 256, 512:1024] = product(rows[0], up_w[...]).astype(BF)
        part[at : at + 256, 1024:] = product_nt(rows[1], down_w[...]).astype(BF)


def first_products(mine, theirs, weights, after):
    return pl.pallas_call(
        first_kernel,
        in_specs=[VMEM] * 5 + [ANYWHERE],
        out_specs=[VMEM] * 2,
        out_shape=[
            jax.ShapeDtypeStruct((512, 1536), BF),
            jax.ShapeDtypeStruct((8, 128), F32),
        ],
        compiler_params=pltpu.CompilerParams(vmem_limit_bytes=8 * 2**20),
        cost_estimate=CHEAP,
        name="first_products",
    )(mine, theirs, *weights, after)


def second_kernel(stream, spot, *refs):
    pieces, (gate_w, up_w, down_w) = refs[:9], refs[9:12]
    full, kept, given = refs[-3:]
    base, row = 512 * stream, 0
    for piece in pieces:
        rows = piece.shape[0]
        block = lax.rem(spot[0] + (row // 64), 8)
        start = pl.multiple_of(base + block * 64 + row % 64, 32)
        full[pl.ds(start, rows), :] = piece[...]
        row += rows
    for at, out in ((base, kept), (base + 256, given)):
        rows = slice(at, at + 256)
        out[0] = product(full[rows, :512], down_w[...]).astype(BF)
        out[1] = (
            product_nt(full[rows, 512:1024], gate_w[...])
            + product_nt(full[rows, 1024:], up_w[...])
        ).astype(BF)


def second_products(stream, spot, pieces, weights, full, after):
    operands = [spot, *pieces, *weights, *full, *after]
    return pl.pallas_call(
        functools.partial(second_kernel, stream),
        in_specs=[pl.BlockSpec(memory_space=pltpu.SMEM)]
        + [VMEM] * (12 + len(full))
        + [ANYWHERE] * len(after),
        out_specs=[VMEM] * 3,
        out_shape=[
            jax.ShapeDtypeStruct((1024, 1536), BF),
            jax.ShapeDtypeStruct((2, 256, 1024), BF),
            jax.ShapeDtypeStruct((2, 256, 1024), BF),
        ],
        input_output_aliases={13: 0} if full else {},
        compiler_params=pltpu.CompilerParams(vmem_limit_bytes=8 * 2**20),
        cost_estimate=CHEAP,
        name="second_products",
    )(*operands)


def sum_kernel(kept, got, first, second):
    first[...] = add(kept[:, :128], got[:, :128]).astype(BF)
    second[...] = add(kept[:, 128:], got[:, 128:]).astype(BF)


def core_sums(kept, got):
    return pl.pallas_call(
        sum_kernel,
        in_specs=[VMEM] * 2,
        out_specs=[VMEM] * 2,
        out_shape=[jax.ShapeDtypeStruct((2, 128, 1024), BF)] * 2,
        compiler_params=pltpu.CompilerParams(vmem_limit_bytes=8 * 2**20),
        cost_estimate=CHEAP,
        name="core_sums",
    )(kept, got)


def line_kernel(own, ahead, behind, across, after, wide, narrow, *outs):
    del after, wide, narrow
    total = add(own[...], ahead[...], behind[...], across[...]).astype(BF)
    for index in range(4):
        outs[index][...] = total[:, 32 * index : 32 * index + 32]


def line_total(own, ahead, behind, across, after, wide, narrow):
    piece = jax.ShapeDtypeStruct((2, 32, 1024), BF)
    return pl.pallas_call(
        line_kernel,
        in_specs=[VMEM] * 4 + [ANYWHERE] + [VMEM] * 2,
        out_specs=[VMEM] * 4,
        out_shape=[piece] * 4,
        compiler_params=pltpu.CompilerParams(vmem_limit_bytes=8 * 2**20),
        cost_estimate=CHEAP,
        name="line_total",
    )(own, ahead, behind, across, after, wide, narrow)


def chip_kernel(own, ahead, across, behind, after, outputs, input_grad):
    del after
    total = add(own[...], ahead[...], across[...], behind[...])
    outputs[...] = total[0] * HIDDEN_SCALE
    input_grad[...] = total[1] * WIDTH_SCALE


def chip_total(own, ahead, across, behind, after):
    return pl.pallas_call(
        chip_kernel,
        in_specs=[VMEM] * 5,
        out_specs=[VMEM] * 2,
        out_shape=[jax.ShapeDtypeStruct((32, 1024), F32)] * 2,
        compiler_params=pltpu.CompilerParams(vmem_limit_bytes=8 * 2**20),
        cost_estimate=CHEAP,
        name="chip_total",
    )(own, ahead, across, behind, after)


def stage_kernel(*refs):
    sources, kept, line, sums = refs[:3], refs[3:6], refs[6], refs[7]
    step = pl.program_id(0)

    @pl.when(step == 0)
    def _():
        sums[...] = jnp.zeros_like(sums)

    for slot in range(3):
        source, target = sources[slot], kept[slot]
        base = step * source.shape[0]

        def some(index, total, source=source, target=target, base=base):
            rows = pl.ds(pl.multiple_of(index * ROWS, ROWS), ROWS)
            values = source[rows, :]
            target[pl.ds(pl.multiple_of(base + index * ROWS, ROWS), ROWS), :] = values
            return total + folded(values.astype(F32))

        sums[slot] += lax.fori_loop(
            0, source.shape[0] // ROWS, some, jnp.zeros((8, 128), F32)
        )

    @pl.when(step == 3)
    def _():
        line[...] = sums_line(sums)


def staged(arrays):
    return pl.pallas_call(
        stage_kernel,
        grid=(4,),
        in_specs=[pl.BlockSpec((a.shape[0] // 4, a.shape[1]), lambda i: (i, 0)) for a in arrays],
        out_specs=[VMEM] * 4,
        out_shape=[jax.ShapeDtypeStruct(a.shape, a.dtype) for a in arrays]
        + [jax.ShapeDtypeStruct((1, 128), F32)],
        scratch_shapes=[pltpu.VMEM((6, 8, 128), F32)],
        compiler_params=pltpu.CompilerParams(vmem_limit_bytes=8 * 2**20),
        cost_estimate=CHEAP,
        name="staged",
    )(*arrays)


def pair_kernel(first, second, after, out, token):
    del after
    token[...] = jnp.zeros_like(token)
    out[:, :128] = first[...]
    out[:, 128:] = second[...]


def paired(first, second, after):
    return pl.pallas_call(
        pair_kernel,
        in_specs=[VMEM] * 2 + [ANYWHERE],
        out_specs=[VMEM] * 2,
        out_shape=[
            jax.ShapeDtypeStruct((2, 256, 1024), BF),
            jax.ShapeDtypeStruct((8, 128), F32),
        ],
        compiler_params=pltpu.CompilerParams(vmem_limit_bytes=8 * 2**20),
        cost_estimate=CHEAP,
        name="paired",
    )(first, second, after)


def lay_kernel(mine_a, theirs_a, mine_b, theirs_b, after, turned, cots):
    del after
    for at, rows in ((0, mine_a), (256, theirs_a), (512, mine_b), (768, theirs_b)):
        turned[:, at : at + 256] = rows[0].T
        cots[at : at + 256, :] = rows[1]


def laid(tokens, after):
    square = jax.ShapeDtypeStruct((1024, 1024), BF)
    return pl.pallas_call(
        lay_kernel,
        in_specs=[VMEM] * 4 + [ANYWHERE],
        out_specs=[VMEM] * 2,
        out_shape=[square, square],
        compiler_params=pltpu.CompilerParams(vmem_limit_bytes=8 * 2**20),
        cost_estimate=CHEAP,
        name="laid",
    )(*tokens, after)


def moved(raw, scale, weight, first_moment, second_moment):
    first = first_moment.astype(F32) * (0.9 / FIRST_FIX) + raw * (0.1 * scale / FIRST_FIX)
    second = second_moment.astype(F32) * (0.95 / SECOND_FIX) + (raw * raw) * (
        0.05 * scale * scale / SECOND_FIX
    )
    below = second * lax.rsqrt(second) + 1e-06
    inverse = pl.reciprocal(below, approx=True)
    inverse = inverse * (2.0 - below * inverse)
    return first * inverse + 0.1 * weight.astype(F32)


def folded(values):
    squares = values * values
    total = squares[:8]
    for at in range(8, values.shape[0], 8):
        total = total + squares[at : at + 8]
    out = total[:, :128]
    for at in range(128, values.shape[1], 128):
        out = out + total[:, at : at + 128]
    return out


def moved_rows(raw, scale, w, m, v, out, lanes, base, sums, slot):
    def some(index, total):
        rows = pl.ds(pl.multiple_of(index * ROWS, ROWS), ROWS)
        there = pl.ds(pl.multiple_of(base + index * ROWS, ROWS), ROWS)
        update = moved(raw[rows, lanes], scale, w[there, :], m[rows, :], v[rows, :])
        out[there, lanes] = update.astype(BF)
        return total + folded(update)

    sums[slot] += lax.fori_loop(0, raw.shape[0] // ROWS, some, jnp.zeros((8, 128), F32))


def sums_line(sums):
    lane = lax.broadcasted_iota(jnp.int32, (1, 128), 1)
    line = jnp.zeros((1, 128), F32)
    for slot in range(6):
        line = jnp.where(lane == slot, jnp.sum(sums[slot]), line)
    return line


def down_kernel(cots, full, w, m, v, weight_line, out, line, raw, sums):
    step = pl.program_id(0)

    @pl.when(step == 0)
    def _():
        sums[...] = jnp.zeros_like(sums)

    base = pl.multiple_of(step * 256, 256)
    raw[...] = product_tn(full[:, pl.ds(base, 256)], cots[...])
    moved_rows(raw, HIDDEN_SCALE, w, m, v, out, slice(0, 1024), base, sums, 5)

    @pl.when(step == 1)
    def _():
        line[...] = sums_line(sums) + weight_line[...]


def down_update(cots, full, w, m, v, weight_line):
    block = pl.BlockSpec((256, 1024), lambda i: (i, 0))
    return pl.pallas_call(
        down_kernel,
        grid=(2,),
        in_specs=[VMEM] * 3 + [block] * 2 + [VMEM],
        out_specs=[VMEM] * 2,
        out_shape=[
            jax.ShapeDtypeStruct((512, 1024), BF),
            jax.ShapeDtypeStruct((1, 128), F32),
        ],
        scratch_shapes=[pltpu.VMEM((256, 1024), F32), pltpu.VMEM((6, 8, 128), F32)],
        compiler_params=pltpu.CompilerParams(vmem_limit_bytes=10 * 2**20),
        cost_estimate=CHEAP,
        name="down_update",
    )(cots, full, w, m, v, weight_line)


def wide_kernel(
    turned, full, gate_w, up_w, gate_m, gate_v, up_m, up_v,
    down_line, after, out, lines, raw, sums,
):
    del after
    step = pl.program_id(0)

    @pl.when(step == 0)
    def _():
        sums[...] = jnp.zeros_like(sums)

    base = pl.multiple_of(step * 256, 256)
    raw[...] = product(turned[pl.ds(base, 256), :], full[:, 512:])
    moved_rows(raw, WIDTH_SCALE, gate_w, gate_m, gate_v, out, slice(0, 512), base, sums, 3)
    moved_rows(raw, WIDTH_SCALE, up_w, up_m, up_v, out, slice(512, 1024), base, sums, 4)

    @pl.when(step == 3)
    def _():
        lines[...] = jnp.broadcast_to(sums_line(sums) + down_line[...], lines.shape)


def wide_update(turned, full, gate_w, up_w, moments, down_line, after):
    block = pl.BlockSpec((256, 512), lambda i: (i, 0))
    return pl.pallas_call(
        wide_kernel,
        grid=(4,),
        in_specs=[VMEM] * 4 + [block] * 4 + [VMEM, ANYWHERE],
        out_specs=[VMEM] * 2,
        out_shape=[
            jax.ShapeDtypeStruct((1024, 1024), BF),
            jax.ShapeDtypeStruct((256, 128), F32),
        ],
        scratch_shapes=[pltpu.VMEM((256, 1024), F32), pltpu.VMEM((6, 8, 128), F32)],
        compiler_params=pltpu.CompilerParams(vmem_limit_bytes=10 * 2**20),
        cost_estimate=CHEAP,
        name="wide_update",
    )(turned, full, gate_w, up_w, *moments, down_line, after)


def step_kernel(sums, wide, narrow, gate_out, up_out, down_out):
    step = pl.program_id(0)
    tall = pl.ds(pl.multiple_of(step * 256, 256), 256)
    flat = pl.ds(pl.multiple_of(step * 128, 128), 128)
    totals = jnp.sum(sums[...], axis=0, keepdims=True)

    def ratio(slot):
        return jnp.sqrt(totals[:, slot : slot + 1] / (totals[:, slot + 3 : slot + 4] + 1e-06))

    gate_out[...] = (ratio(0) * wide[tall, :512].astype(F32)).astype(BF)
    up_out[...] = (ratio(1) * wide[tall, 512:].astype(F32)).astype(BF)
    down_out[...] = (ratio(2) * narrow[flat, :].astype(F32)).astype(BF)


def steps(sums, wide, narrow):
    tall = pl.BlockSpec((256, 512), lambda i: (i, 0))
    flat = pl.BlockSpec((128, 1024), lambda i: (i, 0))
    return pl.pallas_call(
        step_kernel,
        grid=(4,),
        in_specs=[VMEM] * 3,
        out_specs=[tall, tall, flat],
        out_shape=[
            jax.ShapeDtypeStruct((1024, 512), BF),
            jax.ShapeDtypeStruct((1024, 512), BF),
            jax.ShapeDtypeStruct((512, 1024), BF),
        ],
        compiler_params=pltpu.CompilerParams(vmem_limit_bytes=8 * 2**20),
        cost_estimate=CHEAP,
        name="steps",
    )(sums, wide, narrow)


def local(
    inputs,
    cotangent,
    gate_weight,
    up_weight,
    down_weight,
    gate_first,
    up_first,
    down_first,
    gate_second,
    up_second,
    down_second,
):
    z = lax.axis_index("col")

    chip = jnp.stack([inputs, cotangent])
    line = jnp.concatenate(
        [chip, along_first(chip, -1), along_first(chip, 2), along_first(chip, 1)], axis=1
    )
    ahead, behind = along_second(line, -1), along_second(line, 1)
    across = along_second(line, 2)

    *weights, weight_line = staged((gate_weight, up_weight, down_weight))
    mine_a, _ = paired(ahead, behind, weight_line)
    mine_b, _ = paired(line, across, weight_line)
    after = weight_line
    mines = [mine_a, mine_b]
    theirs, pieces = [], []
    for mine in mines:
        theirs.append(swap(mine))
        part, after = first_products(mine, theirs[-1], weights, after)
        pieces.append(col_gather(unit_values(*col_scatter(part.reshape(8, 64, 1536), z))))
    spot = jnp.reshape(z, (1,)).astype(jnp.int32)
    full, kept_a, given_a = second_products(
        0, spot, pieces[0], weights, (), (pieces[1][3], pieces[1][6])
    )
    ahead_sum, behind_sum = core_sums(kept_a, swap(given_a))
    turned, cots = laid((mines[0], theirs[0], mines[1], theirs[1]), behind_sum)
    full, kept_b, given_b = second_products(
        1, spot, pieces[1], weights, (full,), (ahead_sum, turned)
    )
    own_sum, across_sum = core_sums(kept_b, swap(given_b))
    narrow, down_line = down_update(cots, full, weights[2], down_first, down_second, weight_line)
    wide, sums = wide_update(
        turned,
        full,
        weights[0],
        weights[1],
        (gate_first, gate_second, up_first, up_second),
        down_line,
        across_sum,
    )
    line_sums = line_total(
        own_sum,
        along_second(ahead_sum, 1),
        along_second(behind_sum, -1),
        along_second(across_sum, 2),
        sums,
        wide,
        narrow,
    )
    spread = lax.all_to_all(sums, ("row", "col"), 0, 0, tiled=True)
    outputs, input_grad = chip_total(
        line_sums[0],
        along_first(line_sums[1], 1),
        along_first(line_sums[2], 2),
        along_first(line_sums[3], -1),
        spread,
    )
    step_gate, step_up, step_down = steps(spread, wide, narrow)
    return (outputs, input_grad, step_gate, step_up, step_down)


def solution(mesh):
    placed = (
        P("row", "col"),
        P("row", "col"),
        P("col", "row"),
        P("col", "row"),
        P("row", "col"),
        P("col", "row"),
        P("col", "row"),
        P("row", "col"),
        P("col", "row"),
        P("col", "row"),
        P("row", "col"),
    )
    return jax.shard_map(
        local,
        mesh=mesh,
        in_specs=placed,
        out_specs=(
            P("row", "col"),
            P("row", "col"),
            P("col", "row"),
            P("col", "row"),
            P("row", "col"),
        ),
        check_vma=False,
    )
```

```python
import functools
import math

import jax
import jax.numpy as jnp
from jax import lax
from jax.experimental import pallas as pl
from jax.experimental.pallas import tpu as pltpu
from jax.sharding import PartitionSpec as P

D = 8192
FF = 16384
FIRST_FIX = 1.0 - 0.9**20
SECOND_FIX = 1.0 - 0.95**20
BF = jnp.bfloat16
F32 = jnp.float32
ROWS = 64
WIDTH_SCALE = 1.0 / math.sqrt(D)
HIDDEN_SCALE = 1.0 / math.sqrt(FF)
ANYWHERE = pl.BlockSpec(memory_space=pl.ANY)
VMEM = pl.BlockSpec(memory_space=pltpu.VMEM)
CHEAP = pl.CostEstimate(flops=0, bytes_accessed=0, transcendentals=0)


def place(y, x, core):
    return ((y % 4) * 4 + (x % 4)) * 2 + core


CHIPS = [(y, x, core) for y in range(4) for x in range(4) for core in range(2)]
SWAP = [(place(y, x, c), place(y, x, 1 - c)) for y, x, c in CHIPS]


def first_axis(step):
    return [
        (place(y, x, c), place(y, x + step, c) if c == 0 else place(y + step, x, c))
        for y, x, c in CHIPS
    ]


def second_axis(step):
    return [
        (place(y, x, c), place(y + step, x, c) if c == 0 else place(y, x + step, c))
        for y, x, c in CHIPS
    ]


def swap(values):
    return lax.ppermute(values, "row", SWAP)


def along_first(values, step):
    return lax.ppermute(values, "row", first_axis(step))


def along_second(values, step):
    return lax.ppermute(values, "row", second_axis(step))


def along_col(values, step):
    return lax.ppermute(values, "col", [(z, (z + step) % 8) for z in range(8)])


def product(left, right):
    return jnp.dot(left, right, preferred_element_type=F32)


def product_nt(left, right):
    return lax.dot_general(left, right, (((1,), (1,)), ((), ())), preferred_element_type=F32)


def product_tn(left, right):
    return lax.dot_general(left, right, (((0,), (0,)), ((), ())), preferred_element_type=F32)


def add(*terms):
    total = terms[0].astype(F32)
    for term in terms[1:]:
        total = total + term.astype(F32)
    return total


def local_grads(gate_value, up_value, grad_hidden):
    sigmoid_gate = jax.nn.sigmoid(gate_value)
    activated = gate_value * sigmoid_gate
    hidden = (activated * up_value).astype(BF)
    d_up = (grad_hidden * activated).astype(BF)
    d_gate = (
        grad_hidden * up_value * sigmoid_gate * (1.0 + gate_value * (1.0 - sigmoid_gate))
    ).astype(BF)
    return (hidden, d_gate, d_up)


def col_scatter(part, z):
    half = part.shape[1] // 2

    def block(offset):
        return lax.dynamic_index_in_dim(part, (z + offset + 8) % 8, 0, keepdims=False)

    far = block(4)
    down = along_col(far[:half], -1)
    up = along_col(far[half:], 1)
    own_down, own_up = block(-3), block(3)
    down = jnp.concatenate([add(down, own_down[:half]).astype(BF), own_down[half:]], axis=0)
    up = jnp.concatenate([own_up[:half], add(up, own_up[half:]).astype(BF)], axis=0)
    for distance in (2, 1):
        down, up = along_col(down, -1), along_col(up, 1)
        down = add(down, block(-distance)).astype(BF)
        up = add(up, block(distance)).astype(BF)
    down, up = along_col(down, -1), along_col(up, 1)
    return block(0), down, up


def col_gather(own):
    half = own.shape[0] // 2
    low, high = [own], [own]
    for _ in range(3):
        low.append(along_col(low[-1], 1))
        high.append(along_col(high[-1], -1))
    far_low, far_high = along_col(low[-1][:half], 1), along_col(high[-1][half:], -1)
    return (own, high[1], high[2], high[3], far_low, far_high, low[3], low[2], low[1])


def value_kernel(own, down, up, out):
    sums = [
        add(own[:, lanes], down[:, lanes], up[:, lanes])
        for lanes in (slice(0, 512), slice(512, 1024), slice(1024, 1536))
    ]
    values = local_grads(sums[0] * WIDTH_SCALE, sums[1] * WIDTH_SCALE, sums[2] * HIDDEN_SCALE)
    for index, value in enumerate(values):
        out[:, 512 * index : 512 * index + 512] = value


def unit_values(own, down, up):
    return pl.pallas_call(
        value_kernel,
        in_specs=[VMEM] * 3,
        out_specs=VMEM,
        out_shape=jax.ShapeDtypeStruct(own.shape, BF),
        compiler_params=pltpu.CompilerParams(vmem_limit_bytes=8 * 2**20),
        cost_estimate=CHEAP,
        name="unit_values",
    )(own, down, up)


def first_kernel(mine, theirs, gate_w, up_w, down_w, after, part, token):
    del after
    token[...] = jnp.zeros_like(token)
    for at, rows in ((0, mine), (256, theirs)):
        part[at : at + 256, :512] = product(rows[0], gate_w[...]).astype(BF)
        part[at : at + 256, 512:1024] = product(rows[0], up_w[...]).astype(BF)
        part[at : at + 256, 1024:] = product_nt(rows[1], down_w[...]).astype(BF)


def first_products(mine, theirs, weights, after):
    return pl.pallas_call(
        first_kernel,
        in_specs=[VMEM] * 5 + [ANYWHERE],
        out_specs=[VMEM] * 2,
        out_shape=[
            jax.ShapeDtypeStruct((512, 1536), BF),
            jax.ShapeDtypeStruct((8, 128), F32),
        ],
        compiler_params=pltpu.CompilerParams(vmem_limit_bytes=8 * 2**20),
        cost_estimate=CHEAP,
        name="first_products",
    )(mine, theirs, *weights, after)


def second_kernel(stream, spot, *refs):
    pieces, (gate_w, up_w, down_w) = refs[:9], refs[9:12]
    full, kept, given = refs[-3:]
    base, row = 512 * stream, 0
    for piece in pieces:
        rows = piece.shape[0]
        block = lax.rem(spot[0] + (row // 64), 8)
        start = pl.multiple_of(base + block * 64 + row % 64, 32)
        full[pl.ds(start, rows), :] = piece[...]
        row += rows
    for at, out in ((base, kept), (base + 256, given)):
        rows = slice(at, at + 256)
        out[0] = product(full[rows, :512], down_w[...]).astype(BF)
        out[1] = (
            product_nt(full[rows, 512:1024], gate_w[...])
            + product_nt(full[rows, 1024:], up_w[...])
        ).astype(BF)


def second_products(stream, spot, pieces, weights, full, after):
    operands = [spot, *pieces, *weights, *full, *after]
    return pl.pallas_call(
        functools.partial(second_kernel, stream),
        in_specs=[pl.BlockSpec(memory_space=pltpu.SMEM)]
        + [VMEM] * (12 + len(full))
        + [ANYWHERE] * len(after),
        out_specs=[VMEM] * 3,
        out_shape=[
            jax.ShapeDtypeStruct((1024, 1536), BF),
            jax.ShapeDtypeStruct((2, 256, 1024), BF),
            jax.ShapeDtypeStruct((2, 256, 1024), BF),
        ],
        input_output_aliases={13: 0} if full else {},
        compiler_params=pltpu.CompilerParams(vmem_limit_bytes=8 * 2**20),
        cost_estimate=CHEAP,
        name="second_products",
    )(*operands)


def sum_kernel(kept, got, first, second):
    first[...] = add(kept[:, :128], got[:, :128]).astype(BF)
    second[...] = add(kept[:, 128:], got[:, 128:]).astype(BF)


def core_sums(kept, got):
    return pl.pallas_call(
        sum_kernel,
        in_specs=[VMEM] * 2,
        out_specs=[VMEM] * 2,
        out_shape=[jax.ShapeDtypeStruct((2, 128, 1024), BF)] * 2,
        compiler_params=pltpu.CompilerParams(vmem_limit_bytes=8 * 2**20),
        cost_estimate=CHEAP,
        name="core_sums",
    )(kept, got)


def line_kernel(own, ahead, behind, across, after, wide, narrow, *outs):
    del after, wide, narrow
    total = add(own[...], ahead[...], behind[...], across[...]).astype(BF)
    for index in range(4):
        outs[index][...] = total[:, 32 * index : 32 * index + 32]


def line_total(own, ahead, behind, across, after, wide, narrow):
    piece = jax.ShapeDtypeStruct((2, 32, 1024), BF)
    return pl.pallas_call(
        line_kernel,
        in_specs=[VMEM] * 4 + [ANYWHERE] + [VMEM] * 2,
        out_specs=[VMEM] * 4,
        out_shape=[piece] * 4,
        compiler_params=pltpu.CompilerParams(vmem_limit_bytes=8 * 2**20),
        cost_estimate=CHEAP,
        name="line_total",
    )(own, ahead, behind, across, after, wide, narrow)


def chip_kernel(own, ahead, across, behind, after, outputs, input_grad):
    del after
    total = add(own[...], ahead[...], across[...], behind[...])
    outputs[...] = total[0] * HIDDEN_SCALE
    input_grad[...] = total[1] * WIDTH_SCALE


def chip_total(own, ahead, across, behind, after):
    return pl.pallas_call(
        chip_kernel,
        in_specs=[VMEM] * 5,
        out_specs=[VMEM] * 2,
        out_shape=[jax.ShapeDtypeStruct((32, 1024), F32)] * 2,
        compiler_params=pltpu.CompilerParams(vmem_limit_bytes=8 * 2**20),
        cost_estimate=CHEAP,
        name="chip_total",
    )(own, ahead, across, behind, after)


def stage_kernel(*refs):
    sources, kept, line, sums = refs[:3], refs[3:6], refs[6], refs[7]
    step = pl.program_id(0)

    @pl.when(step == 0)
    def _():
        sums[...] = jnp.zeros_like(sums)

    for slot in range(3):
        source, target = sources[slot], kept[slot]
        base = step * source.shape[0]

        def some(index, total, source=source, target=target, base=base):
            rows = pl.ds(pl.multiple_of(index * ROWS, ROWS), ROWS)
            values = source[rows, :]
            target[pl.ds(pl.multiple_of(base + index * ROWS, ROWS), ROWS), :] = values
            return total + folded(values.astype(F32))

        sums[slot] += lax.fori_loop(
            0, source.shape[0] // ROWS, some, jnp.zeros((8, 128), F32)
        )

    @pl.when(step == 3)
    def _():
        line[...] = sums_line(sums)


def staged(arrays):
    return pl.pallas_call(
        stage_kernel,
        grid=(4,),
        in_specs=[pl.BlockSpec((a.shape[0] // 4, a.shape[1]), lambda i: (i, 0)) for a in arrays],
        out_specs=[VMEM] * 4,
        out_shape=[jax.ShapeDtypeStruct(a.shape, a.dtype) for a in arrays]
        + [jax.ShapeDtypeStruct((1, 128), F32)],
        scratch_shapes=[pltpu.VMEM((6, 8, 128), F32)],
        compiler_params=pltpu.CompilerParams(vmem_limit_bytes=8 * 2**20),
        cost_estimate=CHEAP,
        name="staged",
    )(*arrays)


def pair_kernel(first, second, after, out, token):
    del after
    token[...] = jnp.zeros_like(token)
    out[:, :128] = first[...]
    out[:, 128:] = second[...]


def paired(first, second, after):
    return pl.pallas_call(
        pair_kernel,
        in_specs=[VMEM] * 2 + [ANYWHERE],
        out_specs=[VMEM] * 2,
        out_shape=[
            jax.ShapeDtypeStruct((2, 256, 1024), BF),
            jax.ShapeDtypeStruct((8, 128), F32),
        ],
        compiler_params=pltpu.CompilerParams(vmem_limit_bytes=8 * 2**20),
        cost_estimate=CHEAP,
        name="paired",
    )(first, second, after)


def lay_kernel(mine_a, theirs_a, mine_b, theirs_b, after, turned, cots):
    del after
    for at, rows in ((0, mine_a), (256, theirs_a), (512, mine_b), (768, theirs_b)):
        turned[:, at : at + 256] = rows[0].T
        cots[at : at + 256, :] = rows[1]


def laid(tokens, after):
    square = jax.ShapeDtypeStruct((1024, 1024), BF)
    return pl.pallas_call(
        lay_kernel,
        in_specs=[VMEM] * 4 + [ANYWHERE],
        out_specs=[VMEM] * 2,
        out_shape=[square, square],
        compiler_params=pltpu.CompilerParams(vmem_limit_bytes=8 * 2**20),
        cost_estimate=CHEAP,
        name="laid",
    )(*tokens, after)


def moved(raw, scale, weight, first_moment, second_moment):
    first = first_moment.astype(F32) * (0.9 / FIRST_FIX) + raw * (0.1 * scale / FIRST_FIX)
    second = second_moment.astype(F32) * (0.95 / SECOND_FIX) + (raw * raw) * (
        0.05 * scale * scale / SECOND_FIX
    )
    below = second * lax.rsqrt(second) + 1e-06
    inverse = pl.reciprocal(below, approx=True)
    inverse = inverse * (2.0 - below * inverse)
    return first * inverse + 0.1 * weight.astype(F32)


def folded(values):
    squares = values * values
    total = squares[:8]
    for at in range(8, values.shape[0], 8):
        total = total + squares[at : at + 8]
    out = total[:, :128]
    for at in range(128, values.shape[1], 128):
        out = out + total[:, at : at + 128]
    return out


def moved_rows(raw, scale, w, m, v, out, lanes, base, sums, slot):
    def some(index, total):
        rows = pl.ds(pl.multiple_of(index * ROWS, ROWS), ROWS)
        there = pl.ds(pl.multiple_of(base + index * ROWS, ROWS), ROWS)
        update = moved(raw[rows, lanes], scale, w[there, :], m[rows, :], v[rows, :])
        out[there, lanes] = update.astype(BF)
        return total + folded(update)

    sums[slot] += lax.fori_loop(0, raw.shape[0] // ROWS, some, jnp.zeros((8, 128), F32))


def sums_line(sums):
    lane = lax.broadcasted_iota(jnp.int32, (1, 128), 1)
    line = jnp.zeros((1, 128), F32)
    for slot in range(6):
        line = jnp.where(lane == slot, jnp.sum(sums[slot]), line)
    return line


def down_kernel(cots, full, w, m, v, weight_line, out, line, raw, sums):
    step = pl.program_id(0)

    @pl.when(step == 0)
    def _():
        sums[...] = jnp.zeros_like(sums)

    base = pl.multiple_of(step * 256, 256)
    raw[...] = product_tn(full[:, pl.ds(base, 256)], cots[...])
    moved_rows(raw, HIDDEN_SCALE, w, m, v, out, slice(0, 1024), base, sums, 5)

    @pl.when(step == 1)
    def _():
        line[...] = sums_line(sums) + weight_line[...]


def down_update(cots, full, w, m, v, weight_line):
    block = pl.BlockSpec((256, 1024), lambda i: (i, 0))
    return pl.pallas_call(
        down_kernel,
        grid=(2,),
        in_specs=[VMEM] * 3 + [block] * 2 + [VMEM],
        out_specs=[VMEM] * 2,
        out_shape=[
            jax.ShapeDtypeStruct((512, 1024), BF),
            jax.ShapeDtypeStruct((1, 128), F32),
        ],
        scratch_shapes=[pltpu.VMEM((256, 1024), F32), pltpu.VMEM((6, 8, 128), F32)],
        compiler_params=pltpu.CompilerParams(vmem_limit_bytes=10 * 2**20),
        cost_estimate=CHEAP,
        name="down_update",
    )(cots, full, w, m, v, weight_line)


def wide_kernel(
    turned, full, gate_w, up_w, gate_m, gate_v, up_m, up_v,
    down_line, after, out, lines, raw, sums,
):
    del after
    step = pl.program_id(0)

    @pl.when(step == 0)
    def _():
        sums[...] = jnp.zeros_like(sums)

    base = pl.multiple_of(step * 256, 256)
    raw[...] = product(turned[pl.ds(base, 256), :], full[:, 512:])
    moved_rows(raw, WIDTH_SCALE, gate_w, gate_m, gate_v, out, slice(0, 512), base, sums, 3)
    moved_rows(raw, WIDTH_SCALE, up_w, up_m, up_v, out, slice(512, 1024), base, sums, 4)

    @pl.when(step == 3)
    def _():
        lines[...] = jnp.broadcast_to(sums_line(sums) + down_line[...], lines.shape)


def wide_update(turned, full, gate_w, up_w, moments, down_line, after):
    block = pl.BlockSpec((256, 512), lambda i: (i, 0))
    return pl.pallas_call(
        wide_kernel,
        grid=(4,),
        in_specs=[VMEM] * 4 + [block] * 4 + [VMEM, ANYWHERE],
        out_specs=[VMEM] * 2,
        out_shape=[
            jax.ShapeDtypeStruct((1024, 1024), BF),
            jax.ShapeDtypeStruct((256, 128), F32),
        ],
        scratch_shapes=[pltpu.VMEM((256, 1024), F32), pltpu.VMEM((6, 8, 128), F32)],
        compiler_params=pltpu.CompilerParams(vmem_limit_bytes=10 * 2**20),
        cost_estimate=CHEAP,
        name="wide_update",
    )(turned, full, gate_w, up_w, *moments, down_line, after)


def step_kernel(sums, wide, narrow, gate_out, up_out, down_out):
    step = pl.program_id(0)
    tall = pl.ds(pl.multiple_of(step * 256, 256), 256)
    flat = pl.ds(pl.multiple_of(step * 128, 128), 128)
    totals = jnp.sum(sums[...], axis=0, keepdims=True)

    def ratio(slot):
        return jnp.sqrt(totals[:, slot : slot + 1] / (totals[:, slot + 3 : slot + 4] + 1e-06))

    gate_out[...] = (ratio(0) * wide[tall, :512].astype(F32)).astype(BF)
    up_out[...] = (ratio(1) * wide[tall, 512:].astype(F32)).astype(BF)
    down_out[...] = (ratio(2) * narrow[flat, :].astype(F32)).astype(BF)


def steps(sums, wide, narrow):
    tall = pl.BlockSpec((256, 512), lambda i: (i, 0))
    flat = pl.BlockSpec((128, 1024), lambda i: (i, 0))
    return pl.pallas_call(
        step_kernel,
        grid=(4,),
        in_specs=[VMEM] * 3,
        out_specs=[tall, tall, flat],
        out_shape=[
            jax.ShapeDtypeStruct((1024, 512), BF),
            jax.ShapeDtypeStruct((1024, 512), BF),
            jax.ShapeDtypeStruct((512, 1024), BF),
        ],
        compiler_params=pltpu.CompilerParams(vmem_limit_bytes=8 * 2**20),
        cost_estimate=CHEAP,
        name="steps",
    )(sums, wide, narrow)


def local(
    inputs,
    cotangent,
    gate_weight,
    up_weight,
    down_weight,
    gate_first,
    up_first,
    down_first,
    gate_second,
    up_second,
    down_second,
):
    z = lax.axis_index("col")

    chip = jnp.stack([inputs, cotangent])
    line = jnp.concatenate(
        [chip, along_first(chip, -1), along_first(chip, 2), along_first(chip, 1)], axis=1
    )
    ahead, behind = along_second(line, -1), along_second(line, 1)
    across = along_second(line, 2)

    *weights, weight_line = staged((gate_weight, up_weight, down_weight))
    mine_a, _ = paired(line, across, weight_line)
    mine_b, _ = paired(ahead, behind, weight_line)
    after = weight_line
    mines = [mine_a, mine_b]
    theirs, pieces = [], []
    for mine in mines:
        theirs.append(swap(mine))
        part, after = first_products(mine, theirs[-1], weights, after)
        pieces.append(col_gather(unit_values(*col_scatter(part.reshape(8, 64, 1536), z))))
    spot = jnp.reshape(z, (1,)).astype(jnp.int32)
    full, kept_a, given_a = second_products(
        0, spot, pieces[0], weights, (), (pieces[1][3], pieces[1][6])
    )
    own_sum, across_sum = core_sums(kept_a, swap(given_a))
    turned, cots = laid((mines[0], theirs[0], mines[1], theirs[1]), across_sum)
    full, kept_b, given_b = second_products(
        1, spot, pieces[1], weights, (full,), (own_sum, turned)
    )
    ahead_sum, behind_sum = core_sums(kept_b, swap(given_b))
    narrow, down_line = down_update(cots, full, weights[2], down_first, down_second, weight_line)
    wide, sums = wide_update(
        turned,
        full,
        weights[0],
        weights[1],
        (gate_first, gate_second, up_first, up_second),
        down_line,
        behind_sum,
    )
    line_sums = line_total(
        own_sum,
        along_second(ahead_sum, 1),
        along_second(behind_sum, -1),
        along_second(across_sum, 2),
        sums,
        wide,
        narrow,
    )
    spread = lax.all_to_all(sums, ("row", "col"), 0, 0, tiled=True)
    outputs, input_grad = chip_total(
        line_sums[0],
        along_first(line_sums[1], 1),
        along_first(line_sums[2], 2),
        along_first(line_sums[3], -1),
        spread,
    )
    step_gate, step_up, step_down = steps(spread, wide, narrow)
    return (outputs, input_grad, step_gate, step_up, step_down)


def solution(mesh):
    placed = (
        P("row", "col"),
        P("row", "col"),
        P("col", "row"),
        P("col", "row"),
        P("row", "col"),
        P("col", "row"),
        P("col", "row"),
        P("row", "col"),
        P("col", "row"),
        P("col", "row"),
        P("row", "col"),
    )
    return jax.shard_map(
        local,
        mesh=mesh,
        in_specs=placed,
        out_specs=(
            P("row", "col"),
            P("row", "col"),
            P("col", "row"),
            P("col", "row"),
            P("row", "col"),
        ),
        check_vma=False,
    )
```
